256 devices in a mesh: row: 32 (over x, z), col: 8 (over y, core).
Axes of the slice: x: 4, y: 4, z: 8, core: 2. Of those that a mesh axis runs over, the one named last changes fastest.
Arguments:
- blocks: bfloat16 [32, 8, 256, 128, 128], P('row', 'col'), may hold values from -0.1875 to 0.1875
- block_rows: int32 [32, 8, 256], P('row', 'col'), may hold values from 0 to 255
- block_cols: int32 [32, 8, 256], P('row', 'col'), may hold values from 0 to 255
- counts: int32 [32, 8], P('row', 'col'), may hold values from 85 to 256, as said below
- data: float32 [1048576], P('row'), may hold values from -16 to 16
Outputs:
- solution: float32 [262144], P('col')
- search: float32 [262144], P('col')
- data_basis: float32 [1048576], P('row')
The draws below stay inside these ranges and needn't reach their ends.
Inputs may be any that keep to these rules, and one draw needn't show every extreme that they name: `counts`: every tile has between 85 and 256 live slots; some tile has exactly 256.
All inputs are finite; a program needn't handle non-finite values.
Results may differ from the reference program's by a relative error of at most 0.013.
Values sent between devices are 32-bit elements; how exact they have to be, the bound alone decides.
A program may use at most 64 MiB of HBM per device.

```python
import jax
import jax.numpy as jnp
from jax import lax

BLOCK = 128
TILE_ROWS = 256
TILE_COLS = 256
SLOTS = 256
ITERS = 3
DATA_LEN = 1048576
N_ROW = 32
N_COL = 8


def draw_counts(key, part):
    first, second = jax.random.split(key)
    values = jax.random.randint(first, (N_ROW * N_COL,), SLOTS // 3, SLOTS + 1)
    chosen = jax.random.randint(second, (), 0, N_ROW * N_COL)
    values = jnp.where(jnp.arange(N_ROW * N_COL) == chosen, SLOTS, values)
    return values.reshape(N_ROW, N_COL).astype(jnp.int32)


def draw_data(key, part):
    ramp = 1.0 + 2.0 * jnp.arange(DATA_LEN, dtype=jnp.float32) / (DATA_LEN - 1)
    values = jnp.clip(jax.random.normal(key, (DATA_LEN,), jnp.float32), -5.3, 5.3) * ramp
    return values.astype(jnp.float32)


def set_ends(values, own_key, smallest, largest):
    longest = values.shape.index(max(values.shape))
    spots = []
    for shift in (0, 1):
        where = [jax.random.randint(jax.random.fold_in(own_key, axis), (), 0, length) for axis, length in enumerate(values.shape)]
        where[longest] = (where[longest] + shift) % values.shape[longest]
        spots.append(tuple(where))
    return values.at[spots[0]].set(smallest).at[spots[1]].set(largest)


def steps_of(key, dims, cuts, low, top_value):
    def one(axis_at, blocks):
        draws = jax.random.uniform(jax.random.fold_in(jax.random.fold_in(key, 6), axis_at), (blocks,), jnp.float32, low / len(cuts), top_value / len(cuts))
        return jnp.repeat(jnp.exp(draws), dims[axis_at] // blocks).reshape((-1,) + (1,) * (len(dims) - axis_at - 1))

    level = one(*cuts[0])
    for cut in cuts[1:]:
        level = level * one(*cut)
    return level


def scatter_about(stream_key, shape, width, reach, pieces=(), kind=jnp.bfloat16):
    loudness = steps_of(stream_key, shape, pieces, -0.22, 0.18) if pieces else 1.0
    entries = jax.random.normal(stream_key, shape, jnp.float32) * width * loudness
    return jnp.minimum(jnp.maximum(entries, -reach), reach).astype(kind)


def setup_inputs(seed: int = 0) -> dict:
    arg_keys = jax.random.split(jax.random.key(seed), 6)
    blocks = scatter_about(arg_keys[0], (N_ROW, N_COL, SLOTS, BLOCK, BLOCK), (BLOCK * SLOTS * N_COL // TILE_ROWS) ** -0.5, 0.1875, ((0, 32), (1, 8)))
    block_rows = set_ends(jax.random.randint(arg_keys[1], (N_ROW, N_COL, SLOTS), 0, TILE_ROWS), jax.random.fold_in(arg_keys[1], 1), 0, TILE_ROWS - 1).astype(jnp.int32)
    block_cols = set_ends(jax.random.randint(arg_keys[2], (N_ROW, N_COL, SLOTS), 0, TILE_COLS), jax.random.fold_in(arg_keys[2], 1), 0, TILE_COLS - 1).astype(jnp.int32)
    counts = draw_counts(jax.random.fold_in(arg_keys[5], 71), 0)
    data = draw_data(jax.random.fold_in(arg_keys[5], 71), 0)
    return {"blocks": blocks, "block_rows": block_rows, "block_cols": block_cols, "counts": counts, "data": data}


EPS = 1e-06

def forward(blocks, block_rows, block_cols, counts, vector):
    vec_b = vector.astype(jnp.bfloat16).reshape(N_COL, TILE_COLS, BLOCK)
    slot_ids = jnp.arange(SLOTS, dtype=jnp.int32)

    def one_row(args):
        tile_blocks, rows_r, cols_r, count_r = args
        picked = jax.vmap(lambda piece, index: piece[index])(vec_b, cols_r)
        prod = jnp.einsum('nkij,nkj->nki', tile_blocks.astype(jnp.float32), picked.astype(jnp.float32), precision=lax.Precision.HIGHEST)
        live = (slot_ids[None, :] < count_r[:, None]).astype(jnp.float32)
        prod = prod * live[:, :, None]
        return jax.ops.segment_sum(prod.reshape(-1, BLOCK), rows_r.reshape(-1), num_segments=TILE_ROWS)
    result = lax.map(one_row, (blocks, block_rows, block_cols, counts))
    return result.reshape(-1)

def adjoint(blocks, block_rows, block_cols, counts, vector):
    vec_b = vector.astype(jnp.bfloat16).reshape(N_ROW, TILE_ROWS, BLOCK)
    slot_ids = jnp.arange(SLOTS, dtype=jnp.int32)

    def one_row(total, args):
        tile_blocks, rows_r, cols_r, count_r, piece_r = args
        picked = piece_r[rows_r]
        prod = jnp.einsum('nkij,nki->nkj', tile_blocks.astype(jnp.float32), picked.astype(jnp.float32), precision=lax.Precision.HIGHEST)
        live = (slot_ids[None, :] < count_r[:, None]).astype(jnp.float32)
        prod = prod * live[:, :, None]
        summed = jax.vmap(lambda p, c: jax.ops.segment_sum(p, c, num_segments=TILE_COLS))(prod, cols_r)
        return (total + summed, None)
    start = jnp.zeros((N_COL, TILE_COLS, BLOCK), jnp.float32)
    total, unused = lax.scan(one_row, start, (blocks, block_rows, block_cols, counts, vec_b))
    return total.reshape(-1)

def norm(vector):
    return jnp.sqrt(jnp.sum(vector * vector) + EPS)

def reference(blocks, block_rows, block_cols, counts, data):
    beta = norm(data)
    data_basis = data / beta
    temp = adjoint(blocks, block_rows, block_cols, counts, data_basis)
    alpha = norm(temp)
    model_basis = temp / alpha
    search = model_basis
    solution = jnp.zeros_like(model_basis)
    phibar = beta
    rhobar = alpha
    for step in range(ITERS):
        temp = forward(blocks, block_rows, block_cols, counts, model_basis) - alpha * data_basis
        beta = norm(temp)
        data_basis = temp / beta
        temp = adjoint(blocks, block_rows, block_cols, counts, data_basis) - beta * model_basis
        alpha = norm(temp)
        model_basis = temp / alpha
        rho = jnp.sqrt(rhobar * rhobar + beta * beta)
        cosine = rhobar / rho
        sine = beta / rho
        theta = sine * alpha
        rhobar = -cosine * alpha
        phi = cosine * phibar
        phibar = sine * phibar
        solution = solution + phi / rho * search
        search = model_basis - theta / rho * search
    return (solution, search, data_basis)
```

```python
import jax
import jax.numpy as jnp
from jax import lax
from jax.experimental import pallas as pl
from jax.experimental.pallas import tpu as pltpu
from jax.sharding import PartitionSpec as P

MESH = pl.DeviceIdType.MESH
F32 = jnp.float32
BF16 = jnp.bfloat16
EPS = 1e-06
ITERS = 3
B = 128
NB = 256
NX, NZ, NY, NC = 4, 8, 4, 2
N_ROW = NX * NZ
N_COL = NY * NC
RCH = NB // N_ROW
CCH = NB // N_COL
GROUP = 16


def ring(step, size):
    return min(step, size - step)


ROW_STEPS = sorted(
    ((dx, dz) for dx in range(NX) for dz in range(NZ) if dx or dz),
    key=lambda s: -(ring(s[0], NX) + ring(s[1], NZ)),
)
COL_STEPS = sorted(
    ((dy, dc) for dy in range(NY) for dc in range(NC) if dy or dc),
    key=lambda s: -(2 * ring(s[0], NY) + s[1]),
)


def block_products(blocks_ref, picks, out_ref):
    row = lax.broadcasted_iota(jnp.int32, (GROUP, B), 0)
    half = GROUP // 2
    for g in range(NB // GROUP):
        base = g * GROUP
        mine = picks[base : base + GROUP]
        lhs = jnp.concatenate(
            [jnp.where((row & (half - 1)) == q, mine, 0.0).astype(BF16) for q in range(half)], axis=1
        )
        left = jnp.concatenate([blocks_ref[base + q] for q in range(half)], axis=0)
        right = jnp.concatenate([blocks_ref[base + half + q] for q in range(half)], axis=0)
        rhs = jnp.concatenate([left, right], axis=1)
        res = jnp.dot(lhs, rhs, preferred_element_type=F32)
        out_ref[base : base + GROUP, :] = jnp.where(row < half, res[:, :B], res[:, B:])


def pick_rows(pick, vector):
    return jnp.dot(pick, vector.astype(BF16), preferred_element_type=F32)


def scatter_rows(place, prod):
    high = prod.astype(BF16)
    low = (prod - high.astype(F32)).astype(BF16)
    return jnp.dot(place, high, preferred_element_type=F32) + jnp.dot(
        place, low, preferred_element_type=F32
    )


def lane_squares(vector):
    return jnp.sum(vector * vector, axis=0, keepdims=True)


def norm_of(parts):
    return jnp.sqrt(jnp.sum(parts, axis=(0, 1), keepdims=True) + EPS)


def kernel(
    blocks_hbm, rows_hbm, cols_hbm, counts_ref, data_hbm,
    sol_ref, search_ref, basis_ref,
    blk, blk_t, rows_v, cols_v, pick_r, pick_c, place_r, place_c, prod,
    tb, wb, gsend, grecv, fsend, frecv, asend, arecv, scal,
    in_sem, blk_sem, g_ssem, g_rsem, w_ssem, w_rsem, f_ssem, f_rsem, t_ssem, t_rsem, a_ssem, a_rsem,
):
    r = lax.axis_index("row")
    c = lax.axis_index("col")
    x, z = r // NZ, r % NZ
    y, core = c // NC, c % NC
    row_peers = [((x + dx) % NX) * NZ + (z + dz) % NZ for dx, dz in ROW_STEPS]
    col_peers = [((y + dy) % NY) * NC + (core + dc) % NC for dy, dc in COL_STEPS]

    barrier = pltpu.get_barrier_semaphore()
    for p in row_peers:
        pl.semaphore_signal(barrier, inc=1, device_id=(p, c), device_id_type=MESH)
    for p in col_peers:
        pl.semaphore_signal(barrier, inc=1, device_id=(r, p), device_id_type=MESH)

    small = [
        pltpu.make_async_copy(rows_hbm, rows_v, in_sem.at[0]),
        pltpu.make_async_copy(cols_hbm, cols_v, in_sem.at[1]),
        pltpu.make_async_copy(data_hbm, tb.at[0], in_sem.at[2]),
    ]
    for copy in small:
        copy.start()
    big = pltpu.make_async_copy(blocks_hbm.at[0, 0], blk, blk_sem)
    big.start()
    for copy in small:
        copy.wait()

    count = counts_ref[0, 0]
    sub = lax.broadcasted_iota(jnp.int32, (NB, NB), 0)
    lane = lax.broadcasted_iota(jnp.int32, (NB, NB), 1)
    live = lane < count

    def one_hot(index_ref):
        return (sub == index_ref[...]).astype(F32)

    hot_r = one_hot(rows_v)
    pick_r[...] = hot_r.T.astype(BF16)
    place_r[...] = jnp.where(live, hot_r, 0.0).astype(BF16)
    hot_c = one_hot(cols_v)
    pick_c[...] = hot_c.T.astype(BF16)
    place_c[...] = jnp.where(live, hot_c, 0.0).astype(BF16)
    big.wait()

    def adjoint_part(it):
        vec = tb[it]
        block_products(blk, pick_rows(pick_r[...], vec), prod)
        part = scatter_rows(place_c[...], prod[...])
        gsend[:, :RCH, :] = part.reshape(N_ROW, RCH, B)
        gsend[:, RCH:, :] = jnp.broadcast_to(lane_squares(vec).reshape(1, 1, B), (N_ROW, 1, B))

    def start_adjoint_send(it):
        for j, p in enumerate(row_peers):
            pltpu.make_async_remote_copy(
                gsend.at[p], grecv.at[it, j], g_ssem, g_rsem.at[it], device_id=(p, c), device_id_type=MESH
            ).start()

    def finish_adjoint(it, first):
        got = grecv.at[it, pl.ds(0, N_ROW - 1)]
        pltpu.make_async_copy(got, got, g_rsem.at[it]).wait()
        total = jnp.sum(grecv[it, : N_ROW - 1], axis=0) + gsend[r]
        beta = norm_of(total[RCH:])
        chunk = total[:RCH] / beta
        if not first:
            alpha = scal[it - 1, 0:1, 0:1]
            chunk = chunk - beta * (wb[it - 1, r] / alpha)
        wb[it, r] = chunk
        scal[it, 1:2, :] = jnp.broadcast_to(beta, (1, B))
        for p in row_peers:
            pltpu.make_async_remote_copy(
                wb.at[it, r], wb.at[it, r], w_ssem, w_rsem.at[it], device_id=(p, c), device_id_type=MESH
            ).start()
        sent = gsend.at[pl.ds(0, N_ROW - 1)]
        pltpu.make_async_copy(sent, sent, g_ssem).wait()
        landed = wb.at[it, pl.ds(0, N_ROW - 1)]
        pltpu.make_async_copy(landed, landed, w_rsem.at[it]).wait()
        pltpu.make_async_copy(landed, landed, w_ssem).wait()

    def forward(it):
        vec = wb[it].reshape(NB, B)
        block_products(blk_t, pick_rows(pick_c[...], vec), prod)
        part = scatter_rows(place_r[...], prod[...])
        fsend[:, :CCH, :] = part.reshape(N_COL, CCH, B)
        fsend[:, CCH:, :] = jnp.broadcast_to(lane_squares(vec).reshape(1, 1, B), (N_COL, 1, B))
        for j, p in enumerate(col_peers):
            pltpu.make_async_remote_copy(
                fsend.at[p], frecv.at[it, j], f_ssem, f_rsem.at[it], device_id=(r, p), device_id_type=MESH
            ).start()
        got = frecv.at[it, pl.ds(0, N_COL - 1)]
        pltpu.make_async_copy(got, got, f_rsem.at[it]).wait()
        total = jnp.sum(frecv[it, : N_COL - 1], axis=0) + fsend[c]
        alpha = norm_of(total[CCH:])
        beta = scal[it, 1:2, 0:1]
        mine = pl.ds(pl.multiple_of(c * CCH, CCH), CCH)
        tb[it + 1, mine] = total[:CCH] / alpha - alpha * (tb[it, mine] / beta)
        scal[it, 0:1, :] = jnp.broadcast_to(alpha, (1, B))
        for p in col_peers:
            pltpu.make_async_remote_copy(
                tb.at[it + 1, mine], tb.at[it + 1, mine], t_ssem, t_rsem.at[it],
                device_id=(r, p), device_id_type=MESH,
            ).start()
        pltpu.make_async_copy(
            fsend.at[pl.ds(0, N_COL - 1)], fsend.at[pl.ds(0, N_COL - 1)], f_ssem
        ).wait()
        landed = tb.at[it + 1, pl.ds(0, NB - CCH)]
        pltpu.make_async_copy(landed, landed, t_rsem.at[it]).wait()
        pltpu.make_async_copy(landed, landed, t_ssem).wait()

    adjoint_part(0)
    pl.semaphore_wait(barrier, N_ROW + N_COL - 2)
    start_adjoint_send(0)

    def transpose_block(k, carry):
        blk_t[k] = blk[k].T
        return carry

    lax.fori_loop(0, NB, transpose_block, 0, unroll=8)
    finish_adjoint(0, True)

    def step(it, carry):
        forward(it)
        adjoint_part(it + 1)
        start_adjoint_send(it + 1)
        finish_adjoint(it + 1, False)
        return carry

    lax.fori_loop(0, ITERS, step, 0)

    asend[...] = lane_squares(wb[ITERS].reshape(NB, B))
    for j, p in enumerate(col_peers):
        pltpu.make_async_remote_copy(
            asend, arecv.at[j], a_ssem, a_rsem, device_id=(r, p), device_id_type=MESH
        ).start()

    alphas = [scal[i, 0:1, 0:1] for i in range(ITERS)]
    betas = [scal[i, 1:2, 0:1] for i in range(ITERS + 1)]
    basis_ref[...] = tb[ITERS] / betas[ITERS]
    search = wb[0].reshape(NB, B) / alphas[0]
    answer = jnp.zeros((NB, B), F32)
    phibar, rhobar = betas[0], alphas[0]
    for i in range(ITERS):
        beta = betas[i + 1]
        rho = jnp.sqrt(rhobar * rhobar + beta * beta)
        cosine, sine = rhobar / rho, beta / rho
        phi = cosine * phibar
        phibar = sine * phibar
        answer = answer + (phi / rho) * search
        if i + 1 < ITERS:
            theta = sine * alphas[i + 1]
            rhobar = -cosine * alphas[i + 1]
            search = wb[i + 1].reshape(NB, B) / alphas[i + 1] - (theta / rho) * search
    sol_ref[...] = answer
    pltpu.make_async_copy(arecv, arecv, a_rsem).wait()
    pltpu.make_async_copy(arecv, arecv, a_ssem).wait()
    squares = jnp.sum(arecv[...], axis=0) + asend[...]
    alpha = norm_of(squares)
    search_ref[...] = wb[ITERS].reshape(NB, B) / alpha - (sine * alpha / rho) * search


def per_device(blocks, block_rows, block_cols, counts, data):
    vec = jax.ShapeDtypeStruct((NB, B), F32)
    hbm = pl.BlockSpec(memory_space=pl.ANY)
    vmem = pl.BlockSpec(memory_space=pltpu.VMEM)
    sol, search, basis = pl.pallas_call(
        kernel,
        out_shape=(vec, vec, vec),
        in_specs=[hbm, hbm, hbm, pl.BlockSpec(memory_space=pltpu.SMEM), hbm],
        out_specs=(vmem, vmem, vmem),
        scratch_shapes=[
            pltpu.VMEM((NB, B, B), BF16),
            pltpu.VMEM((NB, B, B), BF16),
            pltpu.VMEM((1, NB), jnp.int32),
            pltpu.VMEM((1, NB), jnp.int32),
            pltpu.VMEM((NB, NB), BF16),
            pltpu.VMEM((NB, NB), BF16),
            pltpu.VMEM((NB, NB), BF16),
            pltpu.VMEM((NB, NB), BF16),
            pltpu.VMEM((NB, B), F32),
            pltpu.VMEM((ITERS + 1, NB, B), F32),
            pltpu.VMEM((ITERS + 1, N_ROW, RCH, B), F32),
            pltpu.VMEM((N_ROW, RCH + 1, B), F32),
            pltpu.VMEM((ITERS + 1, N_ROW, RCH + 1, B), F32),
            pltpu.VMEM((N_COL, CCH + 1, B), F32),
            pltpu.VMEM((ITERS, N_COL, CCH + 1, B), F32),
            pltpu.VMEM((1, B), F32),
            pltpu.VMEM((N_COL - 1, 1, B), F32),
            pltpu.VMEM((ITERS + 1, 8, B), F32),
            pltpu.SemaphoreType.DMA((3,)),
            pltpu.SemaphoreType.DMA,
            pltpu.SemaphoreType.DMA,
            pltpu.SemaphoreType.DMA((ITERS + 1,)),
            pltpu.SemaphoreType.DMA,
            pltpu.SemaphoreType.DMA((ITERS + 1,)),
            pltpu.SemaphoreType.DMA,
            pltpu.SemaphoreType.DMA((ITERS,)),
            pltpu.SemaphoreType.DMA,
            pltpu.SemaphoreType.DMA((ITERS,)),
            pltpu.SemaphoreType.DMA,
            pltpu.SemaphoreType.DMA,
        ],
        compiler_params=pltpu.CompilerParams(
            collective_id=0, has_side_effects=True, vmem_limit_bytes=48 * 1024 * 1024
        ),
        name="lsqr",
    )(blocks, block_rows[0], block_cols[0], counts, data.reshape(NB, B))
    return sol.reshape(-1), search.reshape(-1), basis.reshape(-1)


def solution(mesh):
    return jax.shard_map(
        per_device,
        mesh=mesh,
        in_specs=(
            P("row", "col", None, None, None),
            P("row", "col", None),
            P("row", "col", None),
            P("row", "col"),
            P("row"),
        ),
        out_specs=(P("col"), P("col"), P("row")),
        check_vma=False,
    )
```

```python
import jax
import jax.numpy as jnp
from jax import lax
from jax.experimental import pallas as pl
from jax.experimental.pallas import tpu as pltpu
from jax.sharding import PartitionSpec as P

MESH = pl.DeviceIdType.MESH
F32 = jnp.float32
BF16 = jnp.bfloat16
EPS = 1e-06
ITERS = 3
B = 128
NB = 256
NX, NZ, NY, NC = 4, 8, 4, 2
N_ROW = NX * NZ
N_COL = NY * NC
OWN = N_ROW // 2
RCH = NB // OWN
LOADS = 4
CCH = NB // N_COL
GROUP = 16


def ring(step, size):
    return min(step, size - step)


ROW_STEPS = sorted(
    ((dx, dz) for dx in range(NX) for dz in range(NZ) if dx or dz),
    key=lambda s: -(ring(s[0], NX) + ring(s[1], NZ)),
)


def nearer(step):
    other = ((step[0] + NX // 2) % NX, (step[1] + NZ // 2) % NZ)
    mine = (ring(step[0], NX) + ring(step[1], NZ), step)
    return mine < (ring(other[0], NX) + ring(other[1], NZ), other)


SERVE_STEPS = [s for s in ROW_STEPS if nearer(s)]
COL_STEPS = sorted(
    ((dy, dc) for dy in range(NY) for dc in range(NC) if dy or dc),
    key=lambda s: -(2 * ring(s[0], NY) + s[1]),
)


def chunk_of(x, z):
    upper = x // (NX // 2)
    return (x % (NX // 2)) * NZ + (z + upper * (NZ // 2)) % NZ


def block_products(blocks_ref, picks, out_ref, loads=()):
    row = lax.broadcasted_iota(jnp.int32, (GROUP, B), 0)
    half = GROUP // 2
    for g in range(NB // GROUP):
        base = g * GROUP
        if loads and base % (NB // LOADS) == 0:
            loads[base * LOADS // NB].wait()
        mine = picks[base : base + GROUP]
        lhs = jnp.concatenate(
            [jnp.where((row & (half - 1)) == q, mine, 0.0).astype(BF16) for q in range(half)], axis=1
        )
        left = jnp.concatenate([blocks_ref[base + q] for q in range(half)], axis=0)
        right = jnp.concatenate([blocks_ref[base + half + q] for q in range(half)], axis=0)
        rhs = jnp.concatenate([left, right], axis=1)
        res = jnp.dot(lhs, rhs, preferred_element_type=F32)
        out_ref[base : base + GROUP, :] = jnp.where(row < half, res[:, :B], res[:, B:])


def pick_rows(pick, vector):
    return jnp.dot(pick, vector.astype(BF16), preferred_element_type=F32)


def scatter_rows(place, prod):
    high = prod.astype(BF16)
    low = (prod - high.astype(F32)).astype(BF16)
    return jnp.dot(place, high, preferred_element_type=F32) + jnp.dot(
        place, low, preferred_element_type=F32
    )


def lane_squares(vector):
    return jnp.sum(vector * vector, axis=0, keepdims=True)


def norm_of(parts):
    return jnp.sqrt(jnp.sum(parts, axis=(0, 1), keepdims=True) + EPS)


def kernel(
    blocks_hbm, rows_hbm, cols_hbm, counts_ref, data_hbm,
    out_hbm,
    blk, blk_t, rows_v, cols_v, pick_r, pick_c, place_r, place_c, prod,
    tb, wb, gsend, grecv, fsend, frecv, asend, arecv, scal, out,
    in_sem, blk_sem, g_ssem, g_rsem, w_ssem, w_rsem, f_ssem, f_rsem, t_ssem, t_rsem, a_ssem, a_rsem, out_sem,
):
    r = lax.axis_index("row")
    c = lax.axis_index("col")
    x, z = r // NZ, r % NZ
    y, core = c // NC, c % NC
    row_xz = [((x + dx) % NX, (z + dz) % NZ) for dx, dz in ROW_STEPS]
    row_peers = [px * NZ + pz for px, pz in row_xz]
    served = [((x + dx) % NX) * NZ + (z + dz) % NZ for dx, dz in SERVE_STEPS]
    own = chunk_of(x, z)
    col_peers = [((y + dy) % NY) * NC + (core + dc) % NC for dy, dc in COL_STEPS]

    barrier = pltpu.get_barrier_semaphore()
    for p in row_peers:
        pl.semaphore_signal(barrier, inc=1, device_id=(p, c), device_id_type=MESH)
    for p in col_peers:
        pl.semaphore_signal(barrier, inc=1, device_id=(r, p), device_id_type=MESH)

    small = [
        pltpu.make_async_copy(rows_hbm, rows_v, in_sem.at[0]),
        pltpu.make_async_copy(cols_hbm, cols_v, in_sem.at[1]),
        pltpu.make_async_copy(data_hbm, tb.at[0], in_sem.at[2]),
    ]
    for copy in small:
        copy.start()
    part = NB // LOADS
    loads = [
        pltpu.make_async_copy(
            blocks_hbm.at[0, 0, pl.ds(i * part, part)], blk.at[pl.ds(i * part, part)], blk_sem.at[i]
        )
        for i in range(LOADS)
    ]
    for copy in loads:
        copy.start()
    for copy in small:
        copy.wait()

    count = counts_ref[0, 0]
    sub = lax.broadcasted_iota(jnp.int32, (NB, NB), 0)
    lane = lax.broadcasted_iota(jnp.int32, (NB, NB), 1)
    live = lane < count

    def one_hot(index_ref):
        return (sub == index_ref[...]).astype(F32)

    hot_r = one_hot(rows_v)
    pick_r[...] = hot_r.T.astype(BF16)
    place_r[...] = jnp.where(live, hot_r, 0.0).astype(BF16)
    hot_c = one_hot(cols_v)
    pick_c[...] = hot_c.T.astype(BF16)
    place_c[...] = jnp.where(live, hot_c, 0.0).astype(BF16)

    def adjoint_part(it, loads=()):
        vec = tb[it]
        block_products(blk, pick_rows(pick_r[...], vec), prod, loads)
        part = scatter_rows(place_c[...], prod[...])
        gsend[:, :RCH, :] = part.reshape(OWN, RCH, B)
        gsend[:, RCH:, :] = jnp.broadcast_to(lane_squares(vec).reshape(1, 1, B), (OWN, 1, B))

    def start_adjoint_send(it):
        for p, (px, pz) in zip(row_peers, row_xz):
            pltpu.make_async_remote_copy(
                gsend.at[chunk_of(px, pz)], grecv.at[it, r], g_ssem, g_rsem.at[it], device_id=(p, c), device_id_type=MESH
            ).start()
        grecv[it, r] = gsend[own]

    def finish_adjoint(it, first):
        got = grecv.at[it, pl.ds(0, N_ROW - 1)]
        pltpu.make_async_copy(got, got, g_rsem.at[it]).wait()
        total = jnp.sum(grecv[it], axis=0)
        beta = norm_of(total[RCH:])
        chunk = total[:RCH] / beta
        if not first:
            alpha = scal[it - 1, 0:1, 0:1]
            chunk = chunk - beta * (wb[it - 1, own] / alpha)
        wb[it, own] = chunk
        scal[it, 1:2, :] = jnp.broadcast_to(beta, (1, B))
        for p in served:
            pltpu.make_async_remote_copy(
                wb.at[it, own], wb.at[it, own], w_ssem, w_rsem.at[it], device_id=(p, c), device_id_type=MESH
            ).start()
        pltpu.make_async_copy(got, got, g_ssem).wait()
        landed = wb.at[it, pl.ds(0, OWN - 1)]
        pltpu.make_async_copy(landed, landed, w_rsem.at[it]).wait()
        pltpu.make_async_copy(landed, landed, w_ssem).wait()

    def forward(it):
        vec = wb[it].reshape(NB, B)
        block_products(blk_t, pick_rows(pick_c[...], vec), prod)
        part = scatter_rows(place_r[...], prod[...])
        fsend[:, :CCH, :] = part.reshape(N_COL, CCH, B)
        fsend[:, CCH:, :] = jnp.broadcast_to(lane_squares(vec).reshape(1, 1, B), (N_COL, 1, B))
        for p in col_peers:
            pltpu.make_async_remote_copy(
                fsend.at[p], frecv.at[it, c], f_ssem, f_rsem.at[it], device_id=(r, p), device_id_type=MESH
            ).start()
        frecv[it, c] = fsend[c]
        got = frecv.at[it, pl.ds(0, N_COL - 1)]
        pltpu.make_async_copy(got, got, f_rsem.at[it]).wait()
        total = jnp.sum(frecv[it], axis=0)
        alpha = norm_of(total[CCH:])
        beta = scal[it, 1:2, 0:1]
        mine = pl.ds(pl.multiple_of(c * CCH, CCH), CCH)
        tb[it + 1, mine] = total[:CCH] / alpha - alpha * (tb[it, mine] / beta)
        scal[it, 0:1, :] = jnp.broadcast_to(alpha, (1, B))
        for p in col_peers:
            pltpu.make_async_remote_copy(
                tb.at[it + 1, mine], tb.at[it + 1, mine], t_ssem, t_rsem.at[it],
                device_id=(r, p), device_id_type=MESH,
            ).start()
        pltpu.make_async_copy(
            fsend.at[pl.ds(0, N_COL - 1)], fsend.at[pl.ds(0, N_COL - 1)], f_ssem
        ).wait()
        landed = tb.at[it + 1, pl.ds(0, NB - CCH)]
        pltpu.make_async_copy(landed, landed, t_rsem.at[it]).wait()
        pltpu.make_async_copy(landed, landed, t_ssem).wait()

    adjoint_part(0, loads)
    pl.semaphore_wait(barrier, N_ROW + N_COL - 2)
    start_adjoint_send(0)

    def transpose_block(k, carry):
        blk_t[k] = blk[k].T
        return carry

    lax.fori_loop(0, NB, transpose_block, 0, unroll=8)
    finish_adjoint(0, True)

    def step(it, carry):
        forward(it)
        adjoint_part(it + 1)
        start_adjoint_send(it + 1)
        finish_adjoint(it + 1, False)
        return carry

    lax.fori_loop(0, ITERS, step, 0)

    asend[...] = lane_squares(wb[ITERS].reshape(NB, B))
    for p in col_peers:
        pltpu.make_async_remote_copy(
            asend, arecv.at[c], a_ssem, a_rsem, device_id=(r, p), device_id_type=MESH
        ).start()
    arecv[c] = asend[...]

    alphas = [scal[i, 0:1, 0:1] for i in range(ITERS)]
    betas = [scal[i, 1:2, 0:1] for i in range(ITERS + 1)]
    stores = [pltpu.make_async_copy(out.at[i], out_hbm.at[i], out_sem.at[i]) for i in range(3)]
    out[2] = tb[ITERS] / betas[ITERS]
    stores[2].start()
    search = wb[0].reshape(NB, B) / alphas[0]
    answer = jnp.zeros((NB, B), F32)
    phibar, rhobar = betas[0], alphas[0]
    for i in range(ITERS):
        beta = betas[i + 1]
        rho = jnp.sqrt(rhobar * rhobar + beta * beta)
        cosine, sine = rhobar / rho, beta / rho
        phi = cosine * phibar
        phibar = sine * phibar
        answer = answer + (phi / rho) * search
        if i + 1 < ITERS:
            theta = sine * alphas[i + 1]
            rhobar = -cosine * alphas[i + 1]
            search = wb[i + 1].reshape(NB, B) / alphas[i + 1] - (theta / rho) * search
    out[0] = answer
    stores[0].start()
    others = arecv.at[pl.ds(0, N_COL - 1)]
    pltpu.make_async_copy(others, others, a_rsem).wait()
    pltpu.make_async_copy(others, others, a_ssem).wait()
    squares = jnp.sum(arecv[...], axis=0)
    alpha = norm_of(squares)
    out[1] = wb[ITERS].reshape(NB, B) / alpha - (sine * alpha / rho) * search
    stores[1].start()
    for copy in stores:
        copy.wait()


def per_device(blocks, block_rows, block_cols, counts, data):
    vec = jax.ShapeDtypeStruct((NB, B), F32)
    hbm = pl.BlockSpec(memory_space=pl.ANY)
    out = pl.pallas_call(
        kernel,
        out_shape=jax.ShapeDtypeStruct((3, NB, B), F32),
        in_specs=[hbm, hbm, hbm, pl.BlockSpec(memory_space=pltpu.SMEM), hbm],
        out_specs=hbm,
        scratch_shapes=[
            pltpu.VMEM((NB, B, B), BF16),
            pltpu.VMEM((NB, B, B), BF16),
            pltpu.VMEM((1, NB), jnp.int32),
            pltpu.VMEM((1, NB), jnp.int32),
            pltpu.VMEM((NB, NB), BF16),
            pltpu.VMEM((NB, NB), BF16),
            pltpu.VMEM((NB, NB), BF16),
            pltpu.VMEM((NB, NB), BF16),
            pltpu.VMEM((NB, B), F32),
            pltpu.VMEM((ITERS + 1, NB, B), F32),
            pltpu.VMEM((ITERS + 1, OWN, RCH, B), F32),
            pltpu.VMEM((OWN, RCH + 1, B), F32),
            pltpu.VMEM((ITERS + 1, N_ROW, RCH + 1, B), F32),
            pltpu.VMEM((N_COL, CCH + 1, B), F32),
            pltpu.VMEM((ITERS, N_COL, CCH + 1, B), F32),
            pltpu.VMEM((1, B), F32),
            pltpu.VMEM((N_COL, 1, B), F32),
            pltpu.VMEM((ITERS + 1, 8, B), F32),
            pltpu.VMEM((3, NB, B), F32),
            pltpu.SemaphoreType.DMA((3,)),
            pltpu.SemaphoreType.DMA((LOADS,)),
            pltpu.SemaphoreType.DMA,
            pltpu.SemaphoreType.DMA((ITERS + 1,)),
            pltpu.SemaphoreType.DMA,
            pltpu.SemaphoreType.DMA((ITERS + 1,)),
            pltpu.SemaphoreType.DMA,
            pltpu.SemaphoreType.DMA((ITERS,)),
            pltpu.SemaphoreType.DMA,
            pltpu.SemaphoreType.DMA((ITERS,)),
            pltpu.SemaphoreType.DMA,
            pltpu.SemaphoreType.DMA,
            pltpu.SemaphoreType.DMA((3,)),
        ],
        compiler_params=pltpu.CompilerParams(
            collective_id=0, has_side_effects=True, vmem_limit_bytes=56 * 1024 * 1024
        ),
        name="lsqr",
    )(blocks, block_rows[0], block_cols[0], counts, data.reshape(NB, B))
    return out[0].reshape(-1), out[1].reshape(-1), out[2].reshape(-1)


def solution(mesh):
    return jax.shard_map(
        per_device,
        mesh=mesh,
        in_specs=(
            P("row", "col", None, None, None),
            P("row", "col", None),
            P("row", "col", None),
            P("row", "col"),
            P("row"),
        ),
        out_specs=(P("col"), P("col"), P("row")),
        check_vma=False,
    )
```

```python
import jax
import jax.numpy as jnp
from jax import lax
from jax.experimental import pallas as pl
from jax.experimental.pallas import tpu as pltpu
from jax.sharding import PartitionSpec as P

MESH = pl.DeviceIdType.MESH
F32 = jnp.float32
BF16 = jnp.bfloat16
EPS = 1e-06
ITERS = 3
B = 128
NB = 256
NX, NZ, NY, NC = 4, 8, 4, 2
N_ROW = NX * NZ
N_COL = NY * NC
RCH = NB // N_ROW
LOADS = 4
HALF = NB // NC
GROUP = 16


def ring(step, size):
    return min(step, size - step)


ROW_STEPS = sorted(
    ((dx, dz) for dx in range(NX) for dz in range(NZ) if dx or dz),
    key=lambda s: -(ring(s[0], NX) + ring(s[1], NZ)),
)

COL_STEPS = sorted(
    ((dy, dc) for dy in range(NY) for dc in range(NC) if dy or dc),
    key=lambda s: -(2 * ring(s[0], NY) + s[1]),
)


def block_products(blocks_ref, picks, out_ref, loads=()):
    row = lax.broadcasted_iota(jnp.int32, (GROUP, B), 0)
    half = GROUP // 2
    for g in range(NB // GROUP):
        base = g * GROUP
        if loads and base % (NB // LOADS) == 0:
            loads[base * LOADS // NB].wait()
        mine = picks[base : base + GROUP]
        lhs = jnp.concatenate(
            [jnp.where((row & (half - 1)) == q, mine, 0.0).astype(BF16) for q in range(half)], axis=1
        )
        left = jnp.concatenate([blocks_ref[base + q] for q in range(half)], axis=0)
        right = jnp.concatenate([blocks_ref[base + half + q] for q in range(half)], axis=0)
        rhs = jnp.concatenate([left, right], axis=1)
        res = jnp.dot(lhs, rhs, preferred_element_type=F32)
        out_ref[base : base + GROUP, :] = jnp.where(row < half, res[:, :B], res[:, B:])


def pick_rows(pick, vector):
    return jnp.dot(pick, vector.astype(BF16), preferred_element_type=F32)


def scatter_rows(place, prod):
    high = prod.astype(BF16)
    low = (prod - high.astype(F32)).astype(BF16)
    return jnp.dot(place, high, preferred_element_type=F32) + jnp.dot(
        place, low, preferred_element_type=F32
    )


def lane_squares(vector):
    return jnp.sum(vector * vector, axis=0, keepdims=True)


def norm_of(parts):
    return jnp.sqrt(jnp.sum(parts, axis=(0, 1), keepdims=True) + EPS)


def kernel(
    blocks_hbm, rows_hbm, cols_hbm, counts_ref, data_hbm,
    out_hbm,
    blk, blk_t, rows_v, cols_v, pick_r, pick_c, place_r, place_c, prod,
    tb, wb, gsend, grecv, fsend, frecv, psend, precv, asend, arecv, scal, out,
    in_sem, blk_sem, g_ssem, g_rsem, w_ssem, w_rsem, f_ssem, f_rsem, p_ssem, p_rsem, t_ssem, t_rsem, a_ssem, a_rsem, out_sem,
):
    r = lax.axis_index("row")
    c = lax.axis_index("col")
    x, z = r // NZ, r % NZ
    y, core = c // NC, c % NC
    row_peers = [((x + dx) % NX) * NZ + (z + dz) % NZ for dx, dz in ROW_STEPS]
    twin = y * NC + 1 - core
    y_peers = [((y + dy) % NY) * NC + core for dy in (2, 1, 3)]
    col_peers = [((y + dy) % NY) * NC + (core + dc) % NC for dy, dc in COL_STEPS]

    barrier = pltpu.get_barrier_semaphore()
    for p in row_peers:
        pl.semaphore_signal(barrier, inc=1, device_id=(p, c), device_id_type=MESH)
    for p in col_peers:
        pl.semaphore_signal(barrier, inc=1, device_id=(r, p), device_id_type=MESH)

    small = [
        pltpu.make_async_copy(rows_hbm, rows_v, in_sem.at[0]),
        pltpu.make_async_copy(cols_hbm, cols_v, in_sem.at[1]),
        pltpu.make_async_copy(data_hbm, tb.at[0], in_sem.at[2]),
    ]
    for copy in small:
        copy.start()
    part = NB // LOADS
    loads = [
        pltpu.make_async_copy(
            blocks_hbm.at[0, 0, pl.ds(i * part, part)], blk.at[pl.ds(i * part, part)], blk_sem.at[i]
        )
        for i in range(LOADS)
    ]
    for copy in loads:
        copy.start()
    for copy in small:
        copy.wait()

    count = counts_ref[0, 0]
    sub = lax.broadcasted_iota(jnp.int32, (NB, NB), 0)
    lane = lax.broadcasted_iota(jnp.int32, (NB, NB), 1)
    live = lane < count

    def one_hot(index_ref):
        return (sub == index_ref[...]).astype(F32)

    hot_r = one_hot(rows_v)
    pick_r[...] = hot_r.T.astype(BF16)
    place_r[...] = jnp.where(live, hot_r, 0.0).astype(BF16)
    hot_c = one_hot(cols_v)
    pick_c[...] = hot_c.T.astype(BF16)
    place_c[...] = jnp.where(live, hot_c, 0.0).astype(BF16)

    def adjoint_part(it, loads=()):
        vec = tb[it]
        block_products(blk, pick_rows(pick_r[...], vec), prod, loads)
        part = scatter_rows(place_c[...], prod[...])
        gsend[:, :RCH, :] = part.reshape(N_ROW, RCH, B)
        gsend[:, RCH:, :] = jnp.broadcast_to(lane_squares(vec).reshape(1, 1, B), (N_ROW, 1, B))

    def start_adjoint_send(it):
        for p in row_peers:
            pltpu.make_async_remote_copy(
                gsend.at[p], grecv.at[it, r], g_ssem, g_rsem.at[it], device_id=(p, c), device_id_type=MESH
            ).start()
        grecv[it, r] = gsend[r]

    def finish_adjoint(it, first):
        got = grecv.at[it, pl.ds(0, N_ROW - 1)]
        pltpu.make_async_copy(got, got, g_rsem.at[it]).wait()
        total = jnp.sum(grecv[it], axis=0)
        beta = norm_of(total[RCH:])
        chunk = total[:RCH] / beta
        if not first:
            alpha = scal[it - 1, 0:1, 0:1]
            chunk = chunk - beta * (wb[it - 1, r] / alpha)
        wb[it, r] = chunk
        scal[it, 1:2, :] = jnp.broadcast_to(beta, (1, B))
        for p in row_peers:
            pltpu.make_async_remote_copy(
                wb.at[it, r], wb.at[it, r], w_ssem, w_rsem.at[it], device_id=(p, c), device_id_type=MESH
            ).start()
        pltpu.make_async_copy(got, got, g_ssem).wait()
        landed = wb.at[it, pl.ds(0, N_ROW - 1)]
        pltpu.make_async_copy(landed, landed, w_rsem.at[it]).wait()
        pltpu.make_async_copy(landed, landed, w_ssem).wait()

    def forward(it):
        vec = wb[it].reshape(NB, B)
        block_products(blk_t, pick_rows(pick_c[...], vec), prod)
        part = scatter_rows(place_r[...], prod[...])
        fsend[:, :HALF, :] = part.reshape(NC, HALF, B)
        fsend[:, HALF:, :] = jnp.broadcast_to(lane_squares(vec).reshape(1, 1, B), (NC, 1, B))
        pair = pltpu.make_async_remote_copy(
            fsend.at[1 - core], frecv.at[it], f_ssem, f_rsem.at[it], device_id=(r, twin), device_id_type=MESH
        )
        pair.start()
        pair.wait()
        psend[...] = fsend[core] + frecv[it]
        for p in y_peers:
            pltpu.make_async_remote_copy(
                psend, precv.at[it, y], p_ssem, p_rsem.at[it], device_id=(r, p), device_id_type=MESH
            ).start()
        precv[it, y] = psend[...]
        beta = scal[it, 1:2, 0:1]
        mine = pl.ds(pl.multiple_of(core * HALF, HALF), HALF)
        unit = tb[it, mine] / beta
        got = precv.at[it, pl.ds(0, NY - 1)]
        pltpu.make_async_copy(got, got, p_rsem.at[it]).wait()
        total = jnp.sum(precv[it], axis=0)
        alpha = norm_of(total[HALF:])
        tb[it + 1, mine] = total[:HALF] / alpha - alpha * unit
        done = pltpu.make_async_remote_copy(
            tb.at[it + 1, mine], tb.at[it + 1, mine], t_ssem, t_rsem.at[it],
            device_id=(r, twin), device_id_type=MESH,
        )
        done.start()
        scal[it, 0:1, :] = jnp.broadcast_to(alpha, (1, B))
        pltpu.make_async_copy(got, got, p_ssem).wait()
        done.wait()

    adjoint_part(0, loads)
    pl.semaphore_wait(barrier, N_ROW + N_COL - 2)
    start_adjoint_send(0)

    def transpose_block(k, carry):
        blk_t[k] = blk[k].T
        return carry

    lax.fori_loop(0, NB, transpose_block, 0, unroll=8)
    finish_adjoint(0, True)

    def step(it, carry):
        forward(it)
        adjoint_part(it + 1)
        start_adjoint_send(it + 1)
        finish_adjoint(it + 1, False)
        return carry

    lax.fori_loop(0, ITERS, step, 0)

    asend[...] = lane_squares(wb[ITERS].reshape(NB, B))
    for p in col_peers:
        pltpu.make_async_remote_copy(
            asend, arecv.at[c], a_ssem, a_rsem, device_id=(r, p), device_id_type=MESH
        ).start()
    arecv[c] = asend[...]

    alphas = [scal[i, 0:1, 0:1] for i in range(ITERS)]
    betas = [scal[i, 1:2, 0:1] for i in range(ITERS + 1)]
    stores = [pltpu.make_async_copy(out.at[i], out_hbm.at[i], out_sem.at[i]) for i in range(3)]
    out[2] = tb[ITERS] / betas[ITERS]
    stores[2].start()
    search = wb[0].reshape(NB, B) / alphas[0]
    answer = jnp.zeros((NB, B), F32)
    phibar, rhobar = betas[0], alphas[0]
    for i in range(ITERS):
        beta = betas[i + 1]
        rho = jnp.sqrt(rhobar * rhobar + beta * beta)
        cosine, sine = rhobar / rho, beta / rho
        phi = cosine * phibar
        phibar = sine * phibar
        answer = answer + (phi / rho) * search
        if i + 1 < ITERS:
            theta = sine * alphas[i + 1]
            rhobar = -cosine * alphas[i + 1]
            search = wb[i + 1].reshape(NB, B) / alphas[i + 1] - (theta / rho) * search
    out[0] = answer
    stores[0].start()
    others = arecv.at[pl.ds(0, N_COL - 1)]
    pltpu.make_async_copy(others, others, a_rsem).wait()
    pltpu.make_async_copy(others, others, a_ssem).wait()
    squares = jnp.sum(arecv[...], axis=0)
    alpha = norm_of(squares)
    out[1] = wb[ITERS].reshape(NB, B) / alpha - (sine * alpha / rho) * search
    stores[1].start()
    for copy in stores:
        copy.wait()


def per_device(blocks, block_rows, block_cols, counts, data):
    vec = jax.ShapeDtypeStruct((NB, B), F32)
    hbm = pl.BlockSpec(memory_space=pl.ANY)
    out = pl.pallas_call(
        kernel,
        out_shape=jax.ShapeDtypeStruct((3, NB, B), F32),
        in_specs=[hbm, hbm, hbm, pl.BlockSpec(memory_space=pltpu.SMEM), hbm],
        out_specs=hbm,
        scratch_shapes=[
            pltpu.VMEM((NB, B, B), BF16),
            pltpu.VMEM((NB, B, B), BF16),
            pltpu.VMEM((1, NB), jnp.int32),
            pltpu.VMEM((1, NB), jnp.int32),
            pltpu.VMEM((NB, NB), BF16),
            pltpu.VMEM((NB, NB), BF16),
            pltpu.VMEM((NB, NB), BF16),
            pltpu.VMEM((NB, NB), BF16),
            pltpu.VMEM((NB, B), F32),
            pltpu.VMEM((ITERS + 1, NB, B), F32),
            pltpu.VMEM((ITERS + 1, N_ROW, RCH, B), F32),
            pltpu.VMEM((N_ROW, RCH + 1, B), F32),
            pltpu.VMEM((ITERS + 1, N_ROW, RCH + 1, B), F32),
            pltpu.VMEM((NC, HALF + 1, B), F32),
            pltpu.VMEM((ITERS, HALF + 1, B), F32),
            pltpu.VMEM((HALF + 1, B), F32),
            pltpu.VMEM((ITERS, NY, HALF + 1, B), F32),
            pltpu.VMEM((1, B), F32),
            pltpu.VMEM((N_COL, 1, B), F32),
            pltpu.VMEM((ITERS + 1, 8, B), F32),
            pltpu.VMEM((3, NB, B), F32),
            pltpu.SemaphoreType.DMA((3,)),
            pltpu.SemaphoreType.DMA((LOADS,)),
            pltpu.SemaphoreType.DMA,
            pltpu.SemaphoreType.DMA((ITERS + 1,)),
            pltpu.SemaphoreType.DMA,
            pltpu.SemaphoreType.DMA((ITERS + 1,)),
            pltpu.SemaphoreType.DMA,
            pltpu.SemaphoreType.DMA((ITERS,)),
            pltpu.SemaphoreType.DMA,
            pltpu.SemaphoreType.DMA((ITERS,)),
            pltpu.SemaphoreType.DMA,
            pltpu.SemaphoreType.DMA((ITERS,)),
            pltpu.SemaphoreType.DMA,
            pltpu.SemaphoreType.DMA,
            pltpu.SemaphoreType.DMA((3,)),
        ],
        compiler_params=pltpu.CompilerParams(
            collective_id=0, has_side_effects=True, vmem_limit_bytes=56 * 1024 * 1024
        ),
        name="lsqr",
    )(blocks, block_rows[0], block_cols[0], counts, data.reshape(NB, B))
    return out[0].reshape(-1), out[1].reshape(-1), out[2].reshape(-1)


def solution(mesh):
    return jax.shard_map(
        per_device,
        mesh=mesh,
        in_specs=(
            P("row", "col", None, None, None),
            P("row", "col", None),
            P("row", "col", None),
            P("row", "col"),
            P("row"),
        ),
        out_specs=(P("col"), P("col"), P("row")),
        check_vma=False,
    )
```

```python
import jax
import jax.numpy as jnp
from jax import lax
from jax.experimental import pallas as pl
from jax.experimental.pallas import tpu as pltpu
from jax.sharding import PartitionSpec as P

MESH = pl.DeviceIdType.MESH
F32 = jnp.float32
BF16 = jnp.bfloat16
EPS = 1e-06
ITERS = 3
B = 128
NB = 256
NX, NZ, NY, NC = 4, 8, 4, 2
N_ROW = NX * NZ
N_COL = NY * NC
RCH = NB // N_ROW
LOADS = 8
HALF = NB // NC
GROUP = 16


def ring(step, size):
    return min(step, size - step)


ROW_STEPS = sorted(
    ((dx, dz) for dx in range(NX) for dz in range(NZ) if dx or dz),
    key=lambda s: -(ring(s[0], NX) + ring(s[1], NZ)),
)

COL_STEPS = sorted(
    ((dy, dc) for dy in range(NY) for dc in range(NC) if dy or dc),
    key=lambda s: -(2 * ring(s[0], NY) + s[1]),
)


def block_products(blocks_ref, picks, out_ref, loads=()):
    row = lax.broadcasted_iota(jnp.int32, (GROUP, B), 0)
    half = GROUP // 2
    for g in range(NB // GROUP):
        base = g * GROUP
        if loads and base % (NB // LOADS) == 0:
            loads[base * LOADS // NB].wait()
        mine = picks[base : base + GROUP]
        lhs = jnp.concatenate(
            [jnp.where((row & (half - 1)) == q, mine, 0.0).astype(BF16) for q in range(half)], axis=1
        )
        left = jnp.concatenate([blocks_ref[base + q] for q in range(half)], axis=0)
        right = jnp.concatenate([blocks_ref[base + half + q] for q in range(half)], axis=0)
        rhs = jnp.concatenate([left, right], axis=1)
        res = jnp.dot(lhs, rhs, preferred_element_type=F32)
        out_ref[base : base + GROUP, :] = jnp.where(row < half, res[:, :B], res[:, B:])


def pick_rows(pick, vector):
    return jnp.dot(pick, vector.astype(BF16), preferred_element_type=F32)


def scatter_rows(place, prod):
    high = prod.astype(BF16)
    low = (prod - high.astype(F32)).astype(BF16)
    return jnp.dot(place, high, preferred_element_type=F32) + jnp.dot(
        place, low, preferred_element_type=F32
    )


def lane_squares(vector):
    return jnp.sum(vector * vector, axis=0, keepdims=True)


def norm_of(parts):
    return jnp.sqrt(jnp.sum(parts, axis=(0, 1), keepdims=True) + EPS)


def kernel(
    blocks_hbm, rows_hbm, cols_hbm, counts_ref, data_hbm,
    out_hbm,
    blk, blk_t, rows_v, cols_v, pick_r, pick_c, place_r, place_c, prod,
    tb, wb, gsend, grecv, fsend, frecv, psend, precv, asend, arecv, scal, out,
    in_sem, blk_sem, g_ssem, g_rsem, w_ssem, w_rsem, f_ssem, f_rsem, p_ssem, p_rsem, t_ssem, t_rsem, a_ssem, a_rsem, out_sem,
):
    r = lax.axis_index("row")
    c = lax.axis_index("col")
    x, z = r // NZ, r % NZ
    y, core = c // NC, c % NC
    row_peers = [((x + dx) % NX) * NZ + (z + dz) % NZ for dx, dz in ROW_STEPS]
    twin = y * NC + 1 - core
    y_peers = [((y + dy) % NY) * NC + core for dy in (2, 1, 3)]
    col_peers = [((y + dy) % NY) * NC + (core + dc) % NC for dy, dc in COL_STEPS]

    small = [
        pltpu.make_async_copy(rows_hbm, rows_v, in_sem.at[0]),
        pltpu.make_async_copy(cols_hbm, cols_v, in_sem.at[1]),
        pltpu.make_async_copy(data_hbm, tb.at[0], in_sem.at[2]),
    ]
    for copy in small:
        copy.start()
    part = NB // LOADS
    loads = [
        pltpu.make_async_copy(
            blocks_hbm.at[0, 0, pl.ds(i * part, part)], blk.at[pl.ds(i * part, part)], blk_sem.at[i]
        )
        for i in range(LOADS)
    ]
    for copy in loads:
        copy.start()

    barrier = pltpu.get_barrier_semaphore()
    for p in row_peers:
        pl.semaphore_signal(barrier, inc=1, device_id=(p, c), device_id_type=MESH)
    for p in col_peers:
        pl.semaphore_signal(barrier, inc=1, device_id=(r, p), device_id_type=MESH)

    for copy in small:
        copy.wait()

    count = counts_ref[0, 0]
    sub = lax.broadcasted_iota(jnp.int32, (NB, NB), 0)
    lane = lax.broadcasted_iota(jnp.int32, (NB, NB), 1)
    live = lane < count

    def one_hot(index_ref):
        return (sub == index_ref[...]).astype(F32)

    pick_r[...] = one_hot(rows_v).T.astype(BF16)
    place_c[...] = jnp.where(live, one_hot(cols_v), 0.0).astype(BF16)

    def adjoint_part(it, loads=()):
        vec = tb[it]
        block_products(blk, pick_rows(pick_r[...], vec), prod, loads)
        part = scatter_rows(place_c[...], prod[...])
        gsend[:, :RCH, :] = part.reshape(N_ROW, RCH, B)
        gsend[:, RCH:, :] = jnp.broadcast_to(lane_squares(vec).reshape(1, 1, B), (N_ROW, 1, B))

    def start_adjoint_send(it):
        for p in row_peers:
            pltpu.make_async_remote_copy(
                gsend.at[p], grecv.at[it, r], g_ssem, g_rsem.at[it], device_id=(p, c), device_id_type=MESH
            ).start()
        grecv[it, r] = gsend[r]

    def finish_adjoint(it, first):
        got = grecv.at[it, pl.ds(0, N_ROW - 1)]
        pltpu.make_async_copy(got, got, g_rsem.at[it]).wait()
        total = jnp.sum(grecv[it], axis=0)
        beta = norm_of(total[RCH:])
        chunk = total[:RCH] / beta
        if not first:
            alpha = scal[it - 1, 0:1, 0:1]
            chunk = chunk - beta * (wb[it - 1, r] / alpha)
        wb[it, r] = chunk
        scal[it, 1:2, :] = jnp.broadcast_to(beta, (1, B))
        for p in row_peers:
            pltpu.make_async_remote_copy(
                wb.at[it, r], wb.at[it, r], w_ssem, w_rsem.at[it], device_id=(p, c), device_id_type=MESH
            ).start()
        pltpu.make_async_copy(got, got, g_ssem).wait()
        landed = wb.at[it, pl.ds(0, N_ROW - 1)]
        pltpu.make_async_copy(landed, landed, w_rsem.at[it]).wait()
        pltpu.make_async_copy(landed, landed, w_ssem).wait()

    def forward(it):
        vec = wb[it].reshape(NB, B)
        block_products(blk_t, pick_rows(pick_c[...], vec), prod)
        squares = lane_squares(vec)
        theirs = pl.ds(pl.multiple_of((1 - core) * HALF, HALF), HALF)
        mine = pl.ds(pl.multiple_of(core * HALF, HALF), HALF)
        fsend[:HALF, :] = scatter_rows(place_r[theirs, :], prod[...])
        fsend[HALF:, :] = squares
        pair = pltpu.make_async_remote_copy(
            fsend, frecv.at[it], f_ssem, f_rsem.at[it], device_id=(r, twin), device_id_type=MESH
        )
        pair.start()
        psend[:HALF, :] = scatter_rows(place_r[mine, :], prod[...])
        psend[HALF:, :] = squares
        pair.wait()
        psend[...] = psend[...] + frecv[it]
        for p in y_peers:
            pltpu.make_async_remote_copy(
                psend, precv.at[it, y], p_ssem, p_rsem.at[it], device_id=(r, p), device_id_type=MESH
            ).start()
        precv[it, y] = psend[...]
        beta = scal[it, 1:2, 0:1]
        unit = tb[it, mine] / beta
        got = precv.at[it, pl.ds(0, NY - 1)]
        pltpu.make_async_copy(got, got, p_rsem.at[it]).wait()
        total = jnp.sum(precv[it], axis=0)
        alpha = norm_of(total[HALF:])
        tb[it + 1, mine] = total[:HALF] / alpha - alpha * unit
        done = pltpu.make_async_remote_copy(
            tb.at[it + 1, mine], tb.at[it + 1, mine], t_ssem, t_rsem.at[it],
            device_id=(r, twin), device_id_type=MESH,
        )
        done.start()
        scal[it, 0:1, :] = jnp.broadcast_to(alpha, (1, B))
        pltpu.make_async_copy(got, got, p_ssem).wait()
        done.wait()

    adjoint_part(0, loads)
    pl.semaphore_wait(barrier, N_ROW + N_COL - 2)
    start_adjoint_send(0)

    def transpose_block(k, carry):
        blk_t[k] = blk[k].T
        return carry

    pick_c[...] = one_hot(cols_v).T.astype(BF16)
    place_r[...] = jnp.where(live, one_hot(rows_v), 0.0).astype(BF16)
    lax.fori_loop(0, NB, transpose_block, 0, unroll=16)
    finish_adjoint(0, True)

    def step(it, carry):
        forward(it)
        adjoint_part(it + 1)
        start_adjoint_send(it + 1)
        finish_adjoint(it + 1, False)
        return carry

    lax.fori_loop(0, ITERS, step, 0)

    asend[...] = lane_squares(wb[ITERS].reshape(NB, B))
    for p in col_peers:
        pltpu.make_async_remote_copy(
            asend, arecv.at[c], a_ssem, a_rsem, device_id=(r, p), device_id_type=MESH
        ).start()
    arecv[c] = asend[...]

    alphas = [scal[i, 0:1, 0:1] for i in range(ITERS)]
    betas = [scal[i, 1:2, 0:1] for i in range(ITERS + 1)]
    stores = [pltpu.make_async_copy(out.at[i], out_hbm.at[i], out_sem.at[i]) for i in range(3)]
    out[2] = tb[ITERS] / betas[ITERS]
    stores[2].start()
    search = wb[0].reshape(NB, B) / alphas[0]
    answer = jnp.zeros((NB, B), F32)
    phibar, rhobar = betas[0], alphas[0]
    for i in range(ITERS):
        beta = betas[i + 1]
        rho = jnp.sqrt(rhobar * rhobar + beta * beta)
        cosine, sine = rhobar / rho, beta / rho
        phi = cosine * phibar
        phibar = sine * phibar
        answer = answer + (phi / rho) * search
        if i + 1 < ITERS:
            theta = sine * alphas[i + 1]
            rhobar = -cosine * alphas[i + 1]
            search = wb[i + 1].reshape(NB, B) / alphas[i + 1] - (theta / rho) * search
    out[0] = answer
    stores[0].start()
    others = arecv.at[pl.ds(0, N_COL - 1)]
    pltpu.make_async_copy(others, others, a_rsem).wait()
    pltpu.make_async_copy(others, others, a_ssem).wait()
    squares = jnp.sum(arecv[...], axis=0)
    alpha = norm_of(squares)
    out[1] = wb[ITERS].reshape(NB, B) / alpha - (sine * alpha / rho) * search
    stores[1].start()
    for copy in stores:
        copy.wait()


def hand_out(out_hbm, sol_hbm, search_hbm, basis_hbm, sem):
    copies = [
        pltpu.make_async_copy(out_hbm.at[i], ref, sem.at[i])
        for i, ref in enumerate((sol_hbm, search_hbm, basis_hbm))
    ]
    for copy in copies:
        copy.start()
    for copy in copies:
        copy.wait()


def per_device(blocks, block_rows, block_cols, counts, data):
    vec = jax.ShapeDtypeStruct((NB, B), F32)
    hbm = pl.BlockSpec(memory_space=pl.ANY)
    out = pl.pallas_call(
        kernel,
        out_shape=jax.ShapeDtypeStruct((3, NB, B), F32),
        in_specs=[hbm, hbm, hbm, pl.BlockSpec(memory_space=pltpu.SMEM), hbm],
        out_specs=hbm,
        scratch_shapes=[
            pltpu.VMEM((NB, B, B), BF16),
            pltpu.VMEM((NB, B, B), BF16),
            pltpu.VMEM((1, NB), jnp.int32),
            pltpu.VMEM((1, NB), jnp.int32),
            pltpu.VMEM((NB, NB), BF16),
            pltpu.VMEM((NB, NB), BF16),
            pltpu.VMEM((NB, NB), BF16),
            pltpu.VMEM((NB, NB), BF16),
            pltpu.VMEM((NB, B), F32),
            pltpu.VMEM((ITERS + 1, NB, B), F32),
            pltpu.VMEM((ITERS + 1, N_ROW, RCH, B), F32),
            pltpu.VMEM((N_ROW, RCH + 1, B), F32),
            pltpu.VMEM((ITERS + 1, N_ROW, RCH + 1, B), F32),
            pltpu.VMEM((HALF + 1, B), F32),
            pltpu.VMEM((ITERS, HALF + 1, B), F32),
            pltpu.VMEM((HALF + 1, B), F32),
            pltpu.VMEM((ITERS, NY, HALF + 1, B), F32),
            pltpu.VMEM((1, B), F32),
            pltpu.VMEM((N_COL, 1, B), F32),
            pltpu.VMEM((ITERS + 1, 8, B), F32),
            pltpu.VMEM((3, NB, B), F32),
            pltpu.SemaphoreType.DMA((3,)),
            pltpu.SemaphoreType.DMA((LOADS,)),
            pltpu.SemaphoreType.DMA,
            pltpu.SemaphoreType.DMA((ITERS + 1,)),
            pltpu.SemaphoreType.DMA,
            pltpu.SemaphoreType.DMA((ITERS + 1,)),
            pltpu.SemaphoreType.DMA,
            pltpu.SemaphoreType.DMA((ITERS,)),
            pltpu.SemaphoreType.DMA,
            pltpu.SemaphoreType.DMA((ITERS,)),
            pltpu.SemaphoreType.DMA,
            pltpu.SemaphoreType.DMA((ITERS,)),
            pltpu.SemaphoreType.DMA,
            pltpu.SemaphoreType.DMA,
            pltpu.SemaphoreType.DMA((3,)),
        ],
        compiler_params=pltpu.CompilerParams(
            collective_id=0, has_side_effects=True, vmem_limit_bytes=56 * 1024 * 1024
        ),
        name="lsqr",
    )(blocks, block_rows[0], block_cols[0], counts, data.reshape(NB, B))
    results = pl.pallas_call(
        hand_out,
        out_shape=(vec, vec, vec),
        in_specs=[hbm],
        out_specs=(hbm, hbm, hbm),
        scratch_shapes=[pltpu.SemaphoreType.DMA((3,))],
        compiler_params=pltpu.CompilerParams(vmem_limit_bytes=56 * 1024 * 1024),
        name="hand_out",
    )(out)
    return tuple(a.reshape(-1) for a in results)


def solution(mesh):
    return jax.shard_map(
        per_device,
        mesh=mesh,
        in_specs=(
            P("row", "col", None, None, None),
            P("row", "col", None),
            P("row", "col", None),
            P("row", "col"),
            P("row"),
        ),
        out_specs=(P("col"), P("col"), P("row")),
        check_vma=False,
    )
```

```python
import jax
import jax.numpy as jnp
from jax import lax
from jax.experimental import pallas as pl
from jax.experimental.pallas import tpu as pltpu
from jax.sharding import PartitionSpec as P

MESH = pl.DeviceIdType.MESH
F32 = jnp.float32
BF16 = jnp.bfloat16
EPS = 1e-06
ITERS = 3
B = 128
NB = 256
NX, NZ, NY, NC = 4, 8, 4, 2
N_ROW = NX * NZ
N_COL = NY * NC
RCH = NB // N_ROW
LOADS = 4
HALF = NB // NC
GROUP = 16


def ring(step, size):
    return min(step, size - step)


ROW_STEPS = sorted(
    ((dx, dz) for dx in range(NX) for dz in range(NZ) if dx or dz),
    key=lambda s: -(ring(s[0], NX) + ring(s[1], NZ)),
)

COL_STEPS = sorted(
    ((dy, dc) for dy in range(NY) for dc in range(NC) if dy or dc),
    key=lambda s: -(2 * ring(s[0], NY) + s[1]),
)


def block_products(blocks_ref, picks, out_ref, loads=()):
    row = lax.broadcasted_iota(jnp.int32, (GROUP, B), 0)
    half = GROUP // 2
    for g in range(NB // GROUP):
        base = g * GROUP
        if loads and base % (NB // LOADS) == 0:
            loads[base * LOADS // NB].wait()
        mine = picks[base : base + GROUP]
        lhs = jnp.concatenate(
            [jnp.where((row & (half - 1)) == q, mine, 0.0).astype(BF16) for q in range(half)], axis=1
        )
        left = jnp.concatenate([blocks_ref[base + q] for q in range(half)], axis=0)
        right = jnp.concatenate([blocks_ref[base + half + q] for q in range(half)], axis=0)
        rhs = jnp.concatenate([left, right], axis=1)
        res = jnp.dot(lhs, rhs, preferred_element_type=F32)
        out_ref[base : base + GROUP, :] = jnp.where(row < half, res[:, :B], res[:, B:])


def pick_rows(pick, vector):
    return jnp.dot(pick, vector.astype(BF16), preferred_element_type=F32)


def scatter_rows(place, prod):
    high = prod.astype(BF16)
    low = (prod - high.astype(F32)).astype(BF16)
    return jnp.dot(place, high, preferred_element_type=F32) + jnp.dot(
        place, low, preferred_element_type=F32
    )


def lane_squares(vector):
    return jnp.sum(vector * vector, axis=0, keepdims=True)


def norm_of(parts):
    return jnp.sqrt(jnp.sum(parts, axis=(0, 1), keepdims=True) + EPS)


def kernel(
    blocks_hbm, rows_hbm, cols_hbm, counts_ref, data_hbm,
    out,
    blk, blk_t, rows_v, cols_v, pick_r, pick_c, place_r, place_c, prod,
    tb, wb, gsend, grecv, fsend, frecv, psend, precv, asend, arecv, scal,
    in_sem, blk_sem, g_ssem, g_rsem, w_ssem, w_rsem, f_ssem, f_rsem, p_ssem, p_rsem, t_ssem, t_rsem, a_ssem, a_rsem,
):
    r = lax.axis_index("row")
    c = lax.axis_index("col")
    x, z = r // NZ, r % NZ
    y, core = c // NC, c % NC
    row_peers = [((x + dx) % NX) * NZ + (z + dz) % NZ for dx, dz in ROW_STEPS]
    twin = y * NC + 1 - core
    y_peers = [((y + dy) % NY) * NC + core for dy in (2, 1, 3)]
    col_peers = [((y + dy) % NY) * NC + (core + dc) % NC for dy, dc in COL_STEPS]

    barrier = pltpu.get_barrier_semaphore()
    for p in row_peers:
        pl.semaphore_signal(barrier, inc=1, device_id=(p, c), device_id_type=MESH)
    for p in col_peers:
        pl.semaphore_signal(barrier, inc=1, device_id=(r, p), device_id_type=MESH)

    small = [
        pltpu.make_async_copy(rows_hbm, rows_v, in_sem.at[0]),
        pltpu.make_async_copy(cols_hbm, cols_v, in_sem.at[1]),
        pltpu.make_async_copy(data_hbm, tb.at[0], in_sem.at[2]),
    ]
    for copy in small:
        copy.start()
    part = NB // LOADS
    loads = [
        pltpu.make_async_copy(
            blocks_hbm.at[0, 0, pl.ds(i * part, part)], blk.at[pl.ds(i * part, part)], blk_sem.at[i]
        )
        for i in range(LOADS)
    ]
    for copy in loads:
        copy.start()
    for copy in small:
        copy.wait()

    count = counts_ref[0, 0]
    sub = lax.broadcasted_iota(jnp.int32, (NB, NB), 0)
    lane = lax.broadcasted_iota(jnp.int32, (NB, NB), 1)
    live = lane < count

    def one_hot(index_ref):
        return (sub == index_ref[...]).astype(F32)

    hot_r = one_hot(rows_v)
    pick_r[...] = hot_r.T.astype(BF16)
    place_r[...] = jnp.where(live, hot_r, 0.0).astype(BF16)
    hot_c = one_hot(cols_v)
    pick_c[...] = hot_c.T.astype(BF16)
    place_c[...] = jnp.where(live, hot_c, 0.0).astype(BF16)

    def adjoint_part(it, loads=()):
        vec = tb[it]
        block_products(blk, pick_rows(pick_r[...], vec), prod, loads)
        part = scatter_rows(place_c[...], prod[...])
        gsend[:, :RCH, :] = part.reshape(N_ROW, RCH, B)
        gsend[:, RCH:, :] = jnp.broadcast_to(lane_squares(vec).reshape(1, 1, B), (N_ROW, 1, B))

    def start_adjoint_send(it):
        for p in row_peers:
            pltpu.make_async_remote_copy(
                gsend.at[p], grecv.at[it, r], g_ssem, g_rsem.at[it], device_id=(p, c), device_id_type=MESH
            ).start()
        grecv[it, r] = gsend[r]

    def finish_adjoint(it, first):
        before = None if first else wb[it - 1, r] / scal[it - 1, 0:1, 0:1]
        got = grecv.at[it, pl.ds(0, N_ROW - 1)]
        pltpu.make_async_copy(got, got, g_rsem.at[it]).wait()
        total = jnp.sum(grecv[it], axis=0)
        beta = norm_of(total[RCH:])
        chunk = total[:RCH] / beta
        if not first:
            chunk = chunk - beta * before
        wb[it, r] = chunk
        scal[it, 1:2, :] = jnp.broadcast_to(beta, (1, B))
        for p in row_peers:
            pltpu.make_async_remote_copy(
                wb.at[it, r], wb.at[it, r], w_ssem, w_rsem.at[it], device_id=(p, c), device_id_type=MESH
            ).start()
        pltpu.make_async_copy(got, got, g_ssem).wait()
        landed = wb.at[it, pl.ds(0, N_ROW - 1)]
        pltpu.make_async_copy(landed, landed, w_rsem.at[it]).wait()
        pltpu.make_async_copy(landed, landed, w_ssem).wait()

    def forward(it):
        vec = wb[it].reshape(NB, B)
        block_products(blk_t, pick_rows(pick_c[...], vec), prod)
        part = scatter_rows(place_r[...], prod[...])
        fsend[:, :HALF, :] = part.reshape(NC, HALF, B)
        fsend[:, HALF:, :] = jnp.broadcast_to(lane_squares(vec).reshape(1, 1, B), (NC, 1, B))
        pair = pltpu.make_async_remote_copy(
            fsend.at[1 - core], frecv.at[it], f_ssem, f_rsem.at[it], device_id=(r, twin), device_id_type=MESH
        )
        pair.start()
        pair.wait()
        psend[...] = fsend[core] + frecv[it]
        for p in y_peers:
            pltpu.make_async_remote_copy(
                psend, precv.at[it, y], p_ssem, p_rsem.at[it], device_id=(r, p), device_id_type=MESH
            ).start()
        precv[it, y] = psend[...]
        beta = scal[it, 1:2, 0:1]
        mine = pl.ds(pl.multiple_of(core * HALF, HALF), HALF)
        unit = tb[it, mine] / beta
        got = precv.at[it, pl.ds(0, NY - 1)]
        pltpu.make_async_copy(got, got, p_rsem.at[it]).wait()
        total = jnp.sum(precv[it], axis=0)
        alpha = norm_of(total[HALF:])
        tb[it + 1, mine] = total[:HALF] / alpha - alpha * unit
        done = pltpu.make_async_remote_copy(
            tb.at[it + 1, mine], tb.at[it + 1, mine], t_ssem, t_rsem.at[it],
            device_id=(r, twin), device_id_type=MESH,
        )
        done.start()
        scal[it, 0:1, :] = jnp.broadcast_to(alpha, (1, B))
        pltpu.make_async_copy(got, got, p_ssem).wait()
        done.wait()

    adjoint_part(0, loads)
    pl.semaphore_wait(barrier, N_ROW + N_COL - 2)
    start_adjoint_send(0)

    def transpose_block(k, carry):
        blk_t[k] = blk[k].T
        return carry

    lax.fori_loop(0, NB, transpose_block, 0, unroll=8)
    finish_adjoint(0, True)

    def step(it, carry):
        forward(it)
        adjoint_part(it + 1)
        start_adjoint_send(it + 1)
        finish_adjoint(it + 1, False)
        return carry

    lax.fori_loop(0, ITERS, step, 0)

    asend[...] = lane_squares(wb[ITERS].reshape(NB, B))
    for p in col_peers:
        pltpu.make_async_remote_copy(
            asend, arecv.at[c], a_ssem, a_rsem, device_id=(r, p), device_id_type=MESH
        ).start()
    arecv[c] = asend[...]

    alphas = [scal[i, 0:1, 0:1] for i in range(ITERS)]
    betas = [scal[i, 1:2, 0:1] for i in range(ITERS + 1)]
    out[2] = tb[ITERS] / betas[ITERS]
    search = wb[0].reshape(NB, B) / alphas[0]
    answer = jnp.zeros((NB, B), F32)
    phibar, rhobar = betas[0], alphas[0]
    for i in range(ITERS):
        beta = betas[i + 1]
        rho = jnp.sqrt(rhobar * rhobar + beta * beta)
        cosine, sine = rhobar / rho, beta / rho
        phi = cosine * phibar
        phibar = sine * phibar
        answer = answer + (phi / rho) * search
        if i + 1 < ITERS:
            theta = sine * alphas[i + 1]
            rhobar = -cosine * alphas[i + 1]
            search = wb[i + 1].reshape(NB, B) / alphas[i + 1] - (theta / rho) * search
    out[0] = answer
    others = arecv.at[pl.ds(0, N_COL - 1)]
    pltpu.make_async_copy(others, others, a_rsem).wait()
    pltpu.make_async_copy(others, others, a_ssem).wait()
    squares = jnp.sum(arecv[...], axis=0)
    alpha = norm_of(squares)
    out[1] = wb[ITERS].reshape(NB, B) / alpha - (sine * alpha / rho) * search


def per_device(blocks, block_rows, block_cols, counts, data):
    vec = jax.ShapeDtypeStruct((NB, B), F32)
    hbm = pl.BlockSpec(memory_space=pl.ANY)

    def in_hbm(a):
        return pltpu.with_memory_space_constraint(a, pltpu.HBM)

    out = pl.pallas_call(
        kernel,
        out_shape=jax.ShapeDtypeStruct((3, NB, B), F32),
        in_specs=[hbm, hbm, hbm, pl.BlockSpec(memory_space=pltpu.SMEM), hbm],
        out_specs=pl.BlockSpec(memory_space=pltpu.VMEM),
        scratch_shapes=[
            pltpu.VMEM((NB, B, B), BF16),
            pltpu.VMEM((NB, B, B), BF16),
            pltpu.VMEM((1, NB), jnp.int32),
            pltpu.VMEM((1, NB), jnp.int32),
            pltpu.VMEM((NB, NB), BF16),
            pltpu.VMEM((NB, NB), BF16),
            pltpu.VMEM((NB, NB), BF16),
            pltpu.VMEM((NB, NB), BF16),
            pltpu.VMEM((NB, B), F32),
            pltpu.VMEM((ITERS + 1, NB, B), F32),
            pltpu.VMEM((ITERS + 1, N_ROW, RCH, B), F32),
            pltpu.VMEM((N_ROW, RCH + 1, B), F32),
            pltpu.VMEM((ITERS + 1, N_ROW, RCH + 1, B), F32),
            pltpu.VMEM((NC, HALF + 1, B), F32),
            pltpu.VMEM((ITERS, HALF + 1, B), F32),
            pltpu.VMEM((HALF + 1, B), F32),
            pltpu.VMEM((ITERS, NY, HALF + 1, B), F32),
            pltpu.VMEM((1, B), F32),
            pltpu.VMEM((N_COL, 1, B), F32),
            pltpu.VMEM((ITERS + 1, 8, B), F32),
            pltpu.SemaphoreType.DMA((3,)),
            pltpu.SemaphoreType.DMA((LOADS,)),
            pltpu.SemaphoreType.DMA,
            pltpu.SemaphoreType.DMA((ITERS + 1,)),
            pltpu.SemaphoreType.DMA,
            pltpu.SemaphoreType.DMA((ITERS + 1,)),
            pltpu.SemaphoreType.DMA,
            pltpu.SemaphoreType.DMA((ITERS,)),
            pltpu.SemaphoreType.DMA,
            pltpu.SemaphoreType.DMA((ITERS,)),
            pltpu.SemaphoreType.DMA,
            pltpu.SemaphoreType.DMA((ITERS,)),
            pltpu.SemaphoreType.DMA,
            pltpu.SemaphoreType.DMA,
        ],
        compiler_params=pltpu.CompilerParams(
            collective_id=0, has_side_effects=True, vmem_limit_bytes=53000 * 1024
        ),
        name="lsqr",
    )(blocks, in_hbm(block_rows[0]), in_hbm(block_cols[0]), counts, in_hbm(data.reshape(NB, B)))
    return out[0].reshape(-1), out[1].reshape(-1), out[2].reshape(-1)


def solution(mesh):
    return jax.shard_map(
        per_device,
        mesh=mesh,
        in_specs=(
            P("row", "col", None, None, None),
            P("row", "col", None),
            P("row", "col", None),
            P("row", "col"),
            P("row"),
        ),
        out_specs=(P("col"), P("col"), P("row")),
        check_vma=False,
    )
```

```python
import jax
import jax.numpy as jnp
from jax import lax
from jax.experimental import pallas as pl
from jax.experimental.pallas import tpu as pltpu
from jax.sharding import PartitionSpec as P

MESH = pl.DeviceIdType.MESH
F32 = jnp.float32
BF16 = jnp.bfloat16
EPS = 1e-06
ITERS = 3
B = 128
NB = 256
NX, NZ, NY, NC = 4, 8, 4, 2
N_ROW = NX * NZ
N_COL = NY * NC
RCH = NB // N_ROW
LOADS = 4
HALF = NB // NC
GROUP = 16


def ring(step, size):
    return min(step, size - step)


ROW_STEPS = sorted(
    ((dx, dz) for dx in range(NX) for dz in range(NZ) if dx or dz),
    key=lambda s: -(ring(s[0], NX) + ring(s[1], NZ)),
)

COL_STEPS = sorted(
    ((dy, dc) for dy in range(NY) for dc in range(NC) if dy or dc),
    key=lambda s: -(2 * ring(s[0], NY) + s[1]),
)


def block_products(blocks_ref, picks, out_ref, loads=()):
    row = lax.broadcasted_iota(jnp.int32, (GROUP, B), 0)
    half = GROUP // 2
    for g in range(NB // GROUP):
        base = g * GROUP
        if loads and base % (NB // LOADS) == 0:
            loads[base * LOADS // NB].wait()
        mine = picks[base : base + GROUP]
        lhs = jnp.concatenate(
            [jnp.where((row & (half - 1)) == q, mine, 0.0).astype(BF16) for q in range(half)], axis=1
        )
        left = jnp.concatenate([blocks_ref[base + q] for q in range(half)], axis=0)
        right = jnp.concatenate([blocks_ref[base + half + q] for q in range(half)], axis=0)
        rhs = jnp.concatenate([left, right], axis=1)
        res = jnp.dot(lhs, rhs, preferred_element_type=F32)
        out_ref[base : base + GROUP, :] = jnp.where(row < half, res[:, :B], res[:, B:])


def swap_lanes(a):
    return jnp.concatenate([a[:, B // 2 :], a[:, : B // 2]], axis=1)


def left_lanes(rows):
    return lax.broadcasted_iota(jnp.int32, (rows, B), 1) < B // 2


def halves(vector):
    low, high = vector[:HALF], vector[HALF:]
    left = left_lanes(HALF)
    return jnp.where(left, low, swap_lanes(high)), jnp.where(left, swap_lanes(low), high)


def whole(first, second):
    left = left_lanes(HALF)
    return jnp.where(left, first, swap_lanes(second)), jnp.where(left, swap_lanes(first), second)


def pick_half(pick, packed):
    packed = packed.astype(BF16)
    low = jnp.dot(pick[:, :HALF], packed, preferred_element_type=F32)
    high = jnp.dot(pick[:, HALF:], packed, preferred_element_type=F32)
    mixed = jnp.where(left_lanes(NB), low, high)
    return mixed + swap_lanes(mixed)


def half_adjoint_products(blocks_ref, h, picks, out_ref, add):
    row = lax.broadcasted_iota(jnp.int32, (GROUP, B), 0)
    side = jnp.where(left_lanes(GROUP), 0, 1)
    half = GROUP // 2
    rows = pl.ds(pl.multiple_of(h * (B // 2), B // 2), B // 2)
    for g in range(NB // GROUP):
        base = g * GROUP
        mine = picks[base : base + GROUP]
        lhs = jnp.concatenate(
            [jnp.where((row & (half - 1)) == q + side, mine, 0.0).astype(BF16) for q in range(0, half, 2)], axis=1
        )
        left = jnp.concatenate([blocks_ref[base + q, rows] for q in range(half)], axis=0)
        right = jnp.concatenate([blocks_ref[base + half + q, rows] for q in range(half)], axis=0)
        res = jnp.dot(lhs, jnp.concatenate([left, right], axis=1), preferred_element_type=F32)
        res = jnp.where(row < half, res[:, :B], res[:, B:])
        if add:
            res = res + out_ref[base : base + GROUP, :]
        out_ref[base : base + GROUP, :] = res


def half_forward_products(blk_t, h, picks, out_ref):
    wide = 2 * GROUP
    row = lax.broadcasted_iota(jnp.int32, (wide, B), 0)
    keep = ((lax.broadcasted_iota(jnp.int32, (GROUP, B), 0) < 8) & left_lanes(GROUP)) | (
        (lax.broadcasted_iota(jnp.int32, (GROUP, B), 0) >= 8) & ~left_lanes(GROUP)
    )
    for g in range(NB // wide):
        base = g * wide
        mine = picks[base : base + wide]
        lhs = jnp.concatenate([jnp.where((row & 7) == q, mine, 0.0).astype(BF16) for q in range(8)], axis=1)
        left = jnp.concatenate([blk_t[h, (g * 8 + q) * 2] for q in range(8)], axis=0)
        right = jnp.concatenate([blk_t[h, (g * 8 + q) * 2 + 1] for q in range(8)], axis=0)
        res = jnp.dot(lhs, jnp.concatenate([left, right], axis=1), preferred_element_type=F32)
        out_ref[base : base + GROUP, :] = jnp.where(keep, res[:GROUP, :B], 0.0)
        out_ref[base + GROUP : base + wide, :] = jnp.where(keep, res[GROUP:, B:], 0.0)


def pick_rows(pick, vector):
    return jnp.dot(pick, vector.astype(BF16), preferred_element_type=F32)


def scatter_rows(place, prod):
    high = prod.astype(BF16)
    low = (prod - high.astype(F32)).astype(BF16)
    return jnp.dot(place, high, preferred_element_type=F32) + jnp.dot(
        place, low, preferred_element_type=F32
    )


def lane_squares(vector):
    return jnp.sum(vector * vector, axis=0, keepdims=True)


def norm_of(parts):
    return jnp.sqrt(jnp.sum(parts, axis=(0, 1), keepdims=True) + EPS)


def kernel(
    blocks_hbm, rows_hbm, cols_hbm, counts_ref, data_hbm,
    out,
    blk, blk_t, rows_v, cols_v, pick_r, pick_c, place_r, place_c, prod,
    data, tb, wb, gsend, grecv, fsend, frecv, psend, precv, asend, arecv, scal,
    in_sem, blk_sem, g_ssem, g_rsem, w_ssem, w_rsem, f_ssem, f_rsem, p_ssem, p_rsem, t_ssem, t_rsem, a_ssem, a_rsem,
):
    r = lax.axis_index("row")
    c = lax.axis_index("col")
    x, z = r // NZ, r % NZ
    y, core = c // NC, c % NC
    row_peers = [((x + dx) % NX) * NZ + (z + dz) % NZ for dx, dz in ROW_STEPS]
    twin = y * NC + 1 - core
    y_peers = [((y + dy) % NY) * NC + core for dy in (2, 1, 3)]
    col_peers = [((y + dy) % NY) * NC + (core + dc) % NC for dy, dc in COL_STEPS]

    barrier = pltpu.get_barrier_semaphore()
    for p in row_peers:
        pl.semaphore_signal(barrier, inc=1, device_id=(p, c), device_id_type=MESH)
    for p in col_peers:
        pl.semaphore_signal(barrier, inc=1, device_id=(r, p), device_id_type=MESH)

    small = [
        pltpu.make_async_copy(rows_hbm, rows_v, in_sem.at[0]),
        pltpu.make_async_copy(cols_hbm, cols_v, in_sem.at[1]),
        pltpu.make_async_copy(data_hbm, data, in_sem.at[2]),
    ]
    for copy in small:
        copy.start()
    part = NB // LOADS
    loads = [
        pltpu.make_async_copy(
            blocks_hbm.at[0, 0, pl.ds(i * part, part)], blk.at[pl.ds(i * part, part)], blk_sem.at[i]
        )
        for i in range(LOADS)
    ]
    for copy in loads:
        copy.start()
    for copy in small:
        copy.wait()

    count = counts_ref[0, 0]
    sub = lax.broadcasted_iota(jnp.int32, (NB, NB), 0)
    lane = lax.broadcasted_iota(jnp.int32, (NB, NB), 1)
    live = lane < count

    def one_hot(index_ref):
        return (sub == index_ref[...]).astype(F32)

    hot_r = one_hot(rows_v)
    pick_r[...] = hot_r.T.astype(BF16)
    place_r[...] = jnp.where(live, hot_r, 0.0).astype(BF16)
    hot_c = one_hot(cols_v)
    pick_c[...] = hot_c.T.astype(BF16)
    place_c[...] = jnp.where(live, hot_c, 0.0).astype(BF16)

    def adjoint_place(squares):
        part = scatter_rows(place_c[...], prod[...])
        gsend[:, :RCH, :] = part.reshape(N_ROW, RCH, B)
        gsend[:, RCH:, :] = jnp.broadcast_to(squares.reshape(1, 1, B), (N_ROW, 1, B))

    def start_adjoint_send(it):
        for p in row_peers:
            pltpu.make_async_remote_copy(
                gsend.at[p], grecv.at[it, r], g_ssem, g_rsem.at[it], device_id=(p, c), device_id_type=MESH
            ).start()
        grecv[it, r] = gsend[r]

    def finish_adjoint(it, first):
        before = None if first else wb[it - 1, r] / scal[it - 1, 0:1, 0:1]
        got = grecv.at[it, pl.ds(0, N_ROW - 1)]
        pltpu.make_async_copy(got, got, g_rsem.at[it]).wait()
        total = jnp.sum(grecv[it], axis=0)
        beta = norm_of(total[RCH:])
        chunk = total[:RCH] / beta
        if not first:
            chunk = chunk - beta * before
        wb[it, r] = chunk
        scal[it, 1:2, :] = jnp.broadcast_to(beta, (1, B))
        for p in row_peers:
            pltpu.make_async_remote_copy(
                wb.at[it, r], wb.at[it, r], w_ssem, w_rsem.at[it], device_id=(p, c), device_id_type=MESH
            ).start()
        pltpu.make_async_copy(got, got, g_ssem).wait()
        landed = wb.at[it, pl.ds(0, N_ROW - 1)]
        pltpu.make_async_copy(landed, landed, w_rsem.at[it]).wait()
        pltpu.make_async_copy(landed, landed, w_ssem).wait()

    def forward_half(h, picks):
        half_forward_products(blk_t, h, picks, prod)
        both = scatter_rows(place_r[...], prod[...])
        both = both + swap_lanes(both)
        return jnp.where(left_lanes(HALF), both[:HALF], both[HALF:])

    def forward_and_adjoint(it):
        vec = wb[it].reshape(NB, B)
        picks = pick_rows(pick_c[...], vec)
        squares = lane_squares(vec)
        fsend[:HALF, :] = forward_half(1 - core, picks)
        fsend[HALF:, :] = squares
        pair = pltpu.make_async_remote_copy(
            fsend, frecv.at[it], f_ssem, f_rsem.at[it], device_id=(r, twin), device_id_type=MESH
        )
        pair.start()
        psend[:HALF, :] = forward_half(core, picks)
        psend[HALF:, :] = squares
        pair.wait()
        psend[...] = psend[...] + frecv[it]
        for p in y_peers:
            pltpu.make_async_remote_copy(
                psend, precv.at[it, y], p_ssem, p_rsem.at[it], device_id=(r, p), device_id_type=MESH
            ).start()
        precv[it, y] = psend[...]
        unit = tb[it, core] / scal[it, 1:2, 0:1]
        got = precv.at[it, pl.ds(0, NY - 1)]
        pltpu.make_async_copy(got, got, p_rsem.at[it]).wait()
        total = jnp.sum(precv[it], axis=0)
        alpha = norm_of(total[HALF:])
        tb[it + 1, core] = total[:HALF] / alpha - alpha * unit
        done = pltpu.make_async_remote_copy(
            tb.at[it + 1, core], tb.at[it + 1, core], t_ssem, t_rsem.at[it],
            device_id=(r, twin), device_id_type=MESH,
        )
        done.start()
        scal[it, 0:1, :] = jnp.broadcast_to(alpha, (1, B))
        half_adjoint_products(blk, core, pick_half(pick_r[...], tb[it + 1, core]), prod, False)
        pltpu.make_async_copy(got, got, p_ssem).wait()
        done.wait()
        half_adjoint_products(blk, 1 - core, pick_half(pick_r[...], tb[it + 1, 1 - core]), prod, True)
        adjoint_place(lane_squares(tb[it + 1, 0]) + lane_squares(tb[it + 1, 1]))

    block_products(blk, pick_rows(pick_r[...], data[...]), prod, loads)
    adjoint_place(lane_squares(data[...]))
    pl.semaphore_wait(barrier, N_ROW + N_COL - 2)
    start_adjoint_send(0)
    tb[0, 0], tb[0, 1] = halves(data[...])

    def transpose_pair(n, carry):
        first = (n // 16) * 32 + (n % 2) * 16 + (n // 2) % 8
        for h in range(2):
            rows = slice(h * (B // 2), (h + 1) * (B // 2))
            blk_t[h, n] = jnp.concatenate([blk[first, rows], blk[first + 8, rows]], axis=0).T
        return carry

    lax.fori_loop(0, NB // 2, transpose_pair, 0, unroll=8)
    finish_adjoint(0, True)

    def step(it, carry):
        forward_and_adjoint(it)
        start_adjoint_send(it + 1)
        finish_adjoint(it + 1, False)
        return carry

    lax.fori_loop(0, ITERS, step, 0)

    asend[...] = lane_squares(wb[ITERS].reshape(NB, B))
    for p in col_peers:
        pltpu.make_async_remote_copy(
            asend, arecv.at[c], a_ssem, a_rsem, device_id=(r, p), device_id_type=MESH
        ).start()
    arecv[c] = asend[...]

    alphas = [scal[i, 0:1, 0:1] for i in range(ITERS)]
    betas = [scal[i, 1:2, 0:1] for i in range(ITERS + 1)]
    top, bottom = whole(tb[ITERS, 0] / betas[ITERS], tb[ITERS, 1] / betas[ITERS])
    out[2, :HALF] = top
    out[2, HALF:] = bottom
    search = wb[0].reshape(NB, B) / alphas[0]
    answer = jnp.zeros((NB, B), F32)
    phibar, rhobar = betas[0], alphas[0]
    for i in range(ITERS):
        beta = betas[i + 1]
        rho = jnp.sqrt(rhobar * rhobar + beta * beta)
        cosine, sine = rhobar / rho, beta / rho
        phi = cosine * phibar
        phibar = sine * phibar
        answer = answer + (phi / rho) * search
        if i + 1 < ITERS:
            theta = sine * alphas[i + 1]
            rhobar = -cosine * alphas[i + 1]
            search = wb[i + 1].reshape(NB, B) / alphas[i + 1] - (theta / rho) * search
    out[0] = answer
    others = arecv.at[pl.ds(0, N_COL - 1)]
    pltpu.make_async_copy(others, others, a_rsem).wait()
    pltpu.make_async_copy(others, others, a_ssem).wait()
    squares = jnp.sum(arecv[...], axis=0)
    alpha = norm_of(squares)
    out[1] = wb[ITERS].reshape(NB, B) / alpha - (sine * alpha / rho) * search


def per_device(blocks, block_rows, block_cols, counts, data):
    vec = jax.ShapeDtypeStruct((NB, B), F32)
    hbm = pl.BlockSpec(memory_space=pl.ANY)

    def in_hbm(a):
        return pltpu.with_memory_space_constraint(a, pltpu.HBM)

    out = pl.pallas_call(
        kernel,
        out_shape=jax.ShapeDtypeStruct((3, NB, B), F32),
        in_specs=[hbm, hbm, hbm, pl.BlockSpec(memory_space=pltpu.SMEM), hbm],
        out_specs=pl.BlockSpec(memory_space=pltpu.VMEM),
        scratch_shapes=[
            pltpu.VMEM((NB, B, B), BF16),
            pltpu.VMEM((2, NB // 2, B, B), BF16),
            pltpu.VMEM((1, NB), jnp.int32),
            pltpu.VMEM((1, NB), jnp.int32),
            pltpu.VMEM((NB, NB), BF16),
            pltpu.VMEM((NB, NB), BF16),
            pltpu.VMEM((NB, NB), BF16),
            pltpu.VMEM((NB, NB), BF16),
            pltpu.VMEM((NB, B), F32),
            pltpu.VMEM((NB, B), F32),
            pltpu.VMEM((ITERS + 1, 2, HALF, B), F32),
            pltpu.VMEM((ITERS + 1, N_ROW, RCH, B), F32),
            pltpu.VMEM((N_ROW, RCH + 1, B), F32),
            pltpu.VMEM((ITERS + 1, N_ROW, RCH + 1, B), F32),
            pltpu.VMEM((HALF + 1, B), F32),
            pltpu.VMEM((ITERS, HALF + 1, B), F32),
            pltpu.VMEM((HALF + 1, B), F32),
            pltpu.VMEM((ITERS, NY, HALF + 1, B), F32),
            pltpu.VMEM((1, B), F32),
            pltpu.VMEM((N_COL, 1, B), F32),
            pltpu.VMEM((ITERS + 1, 8, B), F32),
            pltpu.SemaphoreType.DMA((3,)),
            pltpu.SemaphoreType.DMA((LOADS,)),
            pltpu.SemaphoreType.DMA,
            pltpu.SemaphoreType.DMA((ITERS + 1,)),
            pltpu.SemaphoreType.DMA,
            pltpu.SemaphoreType.DMA((ITERS + 1,)),
            pltpu.SemaphoreType.DMA,
            pltpu.SemaphoreType.DMA((ITERS,)),
            pltpu.SemaphoreType.DMA,
            pltpu.SemaphoreType.DMA((ITERS,)),
            pltpu.SemaphoreType.DMA,
            pltpu.SemaphoreType.DMA((ITERS,)),
            pltpu.SemaphoreType.DMA,
            pltpu.SemaphoreType.DMA,
        ],
        compiler_params=pltpu.CompilerParams(
            collective_id=0, has_side_effects=True, vmem_limit_bytes=53000 * 1024
        ),
        name="lsqr",
    )(blocks, in_hbm(block_rows[0]), in_hbm(block_cols[0]), counts, in_hbm(data.reshape(NB, B)))
    return out[0].reshape(-1), out[1].reshape(-1), out[2].reshape(-1)


def solution(mesh):
    return jax.shard_map(
        per_device,
        mesh=mesh,
        in_specs=(
            P("row", "col", None, None, None),
            P("row", "col", None),
            P("row", "col", None),
            P("row", "col"),
            P("row"),
        ),
        out_specs=(P("col"), P("col"), P("row")),
        check_vma=False,
    )
```

```python
import jax
import jax.numpy as jnp
from jax import lax
from jax.experimental import pallas as pl
from jax.experimental.pallas import tpu as pltpu
from jax.sharding import PartitionSpec as P

MESH = pl.DeviceIdType.MESH
F32 = jnp.float32
BF16 = jnp.bfloat16
EPS = 1e-06
ITERS = 3
B = 128
NB = 256
NX, NZ, NY, NC = 4, 8, 4, 2
N_ROW = NX * NZ
N_COL = NY * NC
RCH = NB // N_ROW
LOADS = 4
HALF = NB // NC
GROUP = 16


def ring(step, size):
    return min(step, size - step)


ROW_STEPS = sorted(
    ((dx, dz) for dx in range(NX) for dz in range(NZ) if dx or dz),
    key=lambda s: -(ring(s[0], NX) + ring(s[1], NZ)),
)

COL_STEPS = sorted(
    ((dy, dc) for dy in range(NY) for dc in range(NC) if dy or dc),
    key=lambda s: -(2 * ring(s[0], NY) + s[1]),
)


def block_products(blocks_ref, picks, out_ref, loads=()):
    row = lax.broadcasted_iota(jnp.int32, (GROUP, B), 0)
    half = GROUP // 2
    for g in range(NB // GROUP):
        base = g * GROUP
        if loads and base % (NB // LOADS) == 0:
            loads[base * LOADS // NB].wait()
        mine = picks[base : base + GROUP]
        lhs = jnp.concatenate(
            [jnp.where((row & (half - 1)) == q, mine, 0.0).astype(BF16) for q in range(half)], axis=1
        )
        left = jnp.concatenate([blocks_ref[base + q] for q in range(half)], axis=0)
        right = jnp.concatenate([blocks_ref[base + half + q] for q in range(half)], axis=0)
        rhs = jnp.concatenate([left, right], axis=1)
        res = jnp.dot(lhs, rhs, preferred_element_type=F32)
        out_ref[base : base + GROUP, :] = jnp.where(row < half, res[:, :B], res[:, B:])


def swap_lanes(a):
    return jnp.concatenate([a[:, B // 2 :], a[:, : B // 2]], axis=1)


def left_lanes(rows):
    return lax.broadcasted_iota(jnp.int32, (rows, B), 1) < B // 2


def halves(vector):
    low, high = vector[:HALF], vector[HALF:]
    left = left_lanes(HALF)
    return jnp.where(left, low, swap_lanes(high)), jnp.where(left, swap_lanes(low), high)


def whole(first, second):
    left = left_lanes(HALF)
    return jnp.where(left, first, swap_lanes(second)), jnp.where(left, swap_lanes(first), second)


def pick_half(pick, packed):
    packed = packed.astype(BF16)
    low = jnp.dot(pick[:, :HALF], packed, preferred_element_type=F32)
    high = jnp.dot(pick[:, HALF:], packed, preferred_element_type=F32)
    mixed = jnp.where(left_lanes(NB), low, high)
    return mixed + swap_lanes(mixed)


def half_adjoint_products(blocks_ref, h, picks, out_ref, add):
    row = lax.broadcasted_iota(jnp.int32, (GROUP, B), 0)
    side = jnp.where(left_lanes(GROUP), 0, 1)
    half = GROUP // 2
    rows = pl.ds(pl.multiple_of(h * (B // 2), B // 2), B // 2)
    for g in range(NB // GROUP):
        base = g * GROUP
        mine = picks[base : base + GROUP]
        lhs = jnp.concatenate(
            [jnp.where((row & (half - 1)) == q + side, mine, 0.0).astype(BF16) for q in range(0, half, 2)], axis=1
        )
        left = jnp.concatenate([blocks_ref[base + q, rows] for q in range(half)], axis=0)
        right = jnp.concatenate([blocks_ref[base + half + q, rows] for q in range(half)], axis=0)
        res = jnp.dot(lhs, jnp.concatenate([left, right], axis=1), preferred_element_type=F32)
        res = jnp.where(row < half, res[:, :B], res[:, B:])
        if add:
            res = res + out_ref[base : base + GROUP, :]
        out_ref[base : base + GROUP, :] = res


def half_forward_products(blk_t, h, picks, out_ref):
    wide = 2 * GROUP
    row = lax.broadcasted_iota(jnp.int32, (wide, B), 0)
    keep = ((lax.broadcasted_iota(jnp.int32, (GROUP, B), 0) < 8) & left_lanes(GROUP)) | (
        (lax.broadcasted_iota(jnp.int32, (GROUP, B), 0) >= 8) & ~left_lanes(GROUP)
    )
    for g in range(NB // wide):
        base = g * wide
        mine = picks[base : base + wide]
        lhs = jnp.concatenate([jnp.where((row & 7) == q, mine, 0.0).astype(BF16) for q in range(8)], axis=1)
        left = jnp.concatenate([blk_t[h, (g * 8 + q) * 2] for q in range(8)], axis=0)
        right = jnp.concatenate([blk_t[h, (g * 8 + q) * 2 + 1] for q in range(8)], axis=0)
        res = jnp.dot(lhs, jnp.concatenate([left, right], axis=1), preferred_element_type=F32)
        out_ref[base : base + GROUP, :] = jnp.where(keep, res[:GROUP, :B], 0.0)
        out_ref[base + GROUP : base + wide, :] = jnp.where(keep, res[GROUP:, B:], 0.0)


def pick_rows(pick, vector):
    return jnp.dot(pick, vector.astype(BF16), preferred_element_type=F32)


def scatter_rows(place, prod):
    high = prod.astype(BF16)
    low = (prod - high.astype(F32)).astype(BF16)
    return jnp.dot(place, high, preferred_element_type=F32) + jnp.dot(
        place, low, preferred_element_type=F32
    )


def lane_squares(vector):
    return jnp.sum(vector * vector, axis=0, keepdims=True)


def norm_of(parts):
    return jnp.sqrt(jnp.sum(parts, axis=(0, 1), keepdims=True) + EPS)


def kernel(
    blocks_hbm, rows_hbm, cols_hbm, counts_ref, data_hbm,
    out,
    blk, blk_t, rows_v, cols_v, pick_r, pick_c, place_r, place_c, prod,
    data, tb, wb, gsend, grecv, fsend, frecv, psend, precv, asend, arecv, bsend, brecv, scal,
    in_sem, blk_sem, g_ssem, g_rsem, w_ssem, w_rsem, f_ssem, f_rsem, p_ssem, p_rsem, t_ssem, t_rsem, a_ssem, a_rsem, b_ssem, b_rsem,
):
    r = lax.axis_index("row")
    c = lax.axis_index("col")
    x, z = r // NZ, r % NZ
    y, core = c // NC, c % NC
    row_peers = [((x + dx) % NX) * NZ + (z + dz) % NZ for dx, dz in ROW_STEPS]
    twin = y * NC + 1 - core
    y_peers = [((y + dy) % NY) * NC + core for dy in (2, 1, 3)]
    col_peers = [((y + dy) % NY) * NC + (core + dc) % NC for dy, dc in COL_STEPS]

    barrier = pltpu.get_barrier_semaphore()
    for p in row_peers:
        pl.semaphore_signal(barrier, inc=1, device_id=(p, c), device_id_type=MESH)
    for p in col_peers:
        pl.semaphore_signal(barrier, inc=1, device_id=(r, p), device_id_type=MESH)

    small = [
        pltpu.make_async_copy(rows_hbm, rows_v, in_sem.at[0]),
        pltpu.make_async_copy(cols_hbm, cols_v, in_sem.at[1]),
        pltpu.make_async_copy(data_hbm, data, in_sem.at[2]),
    ]
    for copy in small:
        copy.start()
    part = NB // LOADS
    loads = [
        pltpu.make_async_copy(
            blocks_hbm.at[0, 0, pl.ds(i * part, part)], blk.at[pl.ds(i * part, part)], blk_sem.at[i]
        )
        for i in range(LOADS)
    ]
    for copy in loads:
        copy.start()
    for copy in small:
        copy.wait()

    count = counts_ref[0, 0]
    sub = lax.broadcasted_iota(jnp.int32, (NB, NB), 0)
    lane = lax.broadcasted_iota(jnp.int32, (NB, NB), 1)
    live = lane < count

    def one_hot(index_ref):
        return (sub == index_ref[...]).astype(F32)

    hot_r = one_hot(rows_v)
    pick_r[...] = hot_r.T.astype(BF16)
    place_r[...] = jnp.where(live, hot_r, 0.0).astype(BF16)
    hot_c = one_hot(cols_v)
    pick_c[...] = hot_c.T.astype(BF16)
    place_c[...] = jnp.where(live, hot_c, 0.0).astype(BF16)

    def adjoint_place(squares):
        part = scatter_rows(place_c[...], prod[...])
        gsend[:, :RCH, :] = part.reshape(N_ROW, RCH, B)
        gsend[:, RCH:, :] = jnp.broadcast_to(squares.reshape(1, 1, B), (N_ROW, 1, B))

    def start_adjoint_send(it):
        for p in row_peers:
            pltpu.make_async_remote_copy(
                gsend.at[p], grecv.at[it, r], g_ssem, g_rsem.at[it], device_id=(p, c), device_id_type=MESH
            ).start()
        grecv[it, r] = gsend[r]

    def start_last_norm():
        asend[...] = lane_squares(wb[ITERS, r])
        for p in col_peers:
            pltpu.make_async_remote_copy(
                asend, arecv.at[c], a_ssem, a_rsem, device_id=(r, p), device_id_type=MESH
            ).start()
        arecv[c] = asend[...]
        others = arecv.at[pl.ds(0, N_COL - 1)]
        pltpu.make_async_copy(others, others, a_rsem).wait()
        bsend[...] = jnp.sum(arecv[...], axis=0)
        for p in row_peers:
            pltpu.make_async_remote_copy(
                bsend, brecv.at[r], b_ssem, b_rsem, device_id=(p, c), device_id_type=MESH
            ).start()
        brecv[r] = bsend[...]
        pltpu.make_async_copy(others, others, a_ssem).wait()

    def finish_adjoint(it, first):
        before = None if first else wb[it - 1, r] / scal[it - 1, 0:1, 0:1]
        got = grecv.at[it, pl.ds(0, N_ROW - 1)]
        pltpu.make_async_copy(got, got, g_rsem.at[it]).wait()
        total = jnp.sum(grecv[it], axis=0)
        beta = norm_of(total[RCH:])
        chunk = total[:RCH] / beta
        if not first:
            chunk = chunk - beta * before
        wb[it, r] = chunk
        scal[it, 1:2, :] = jnp.broadcast_to(beta, (1, B))
        for p in row_peers:
            pltpu.make_async_remote_copy(
                wb.at[it, r], wb.at[it, r], w_ssem, w_rsem.at[it], device_id=(p, c), device_id_type=MESH
            ).start()
        if not first:
            pl.when(it == ITERS)(start_last_norm)
        pltpu.make_async_copy(got, got, g_ssem).wait()
        landed = wb.at[it, pl.ds(0, N_ROW - 1)]
        pltpu.make_async_copy(landed, landed, w_rsem.at[it]).wait()
        pltpu.make_async_copy(landed, landed, w_ssem).wait()

    def forward_half(h, picks):
        half_forward_products(blk_t, h, picks, prod)
        both = scatter_rows(place_r[...], prod[...])
        both = both + swap_lanes(both)
        return jnp.where(left_lanes(HALF), both[:HALF], both[HALF:])

    def forward_and_adjoint(it):
        vec = wb[it].reshape(NB, B)
        picks = pick_rows(pick_c[...], vec)
        squares = lane_squares(vec)
        fsend[:HALF, :] = forward_half(1 - core, picks)
        fsend[HALF:, :] = squares
        pair = pltpu.make_async_remote_copy(
            fsend, frecv.at[it], f_ssem, f_rsem.at[it], device_id=(r, twin), device_id_type=MESH
        )
        pair.start()
        psend[:HALF, :] = forward_half(core, picks)
        psend[HALF:, :] = squares
        pair.wait()
        psend[...] = psend[...] + frecv[it]
        for p in y_peers:
            pltpu.make_async_remote_copy(
                psend, precv.at[it, y], p_ssem, p_rsem.at[it], device_id=(r, p), device_id_type=MESH
            ).start()
        precv[it, y] = psend[...]
        unit = tb[it, core] / scal[it, 1:2, 0:1]
        got = precv.at[it, pl.ds(0, NY - 1)]
        pltpu.make_async_copy(got, got, p_rsem.at[it]).wait()
        total = jnp.sum(precv[it], axis=0)
        alpha = norm_of(total[HALF:])
        tb[it + 1, core] = total[:HALF] / alpha - alpha * unit
        done = pltpu.make_async_remote_copy(
            tb.at[it + 1, core], tb.at[it + 1, core], t_ssem, t_rsem.at[it],
            device_id=(r, twin), device_id_type=MESH,
        )
        done.start()
        scal[it, 0:1, :] = jnp.broadcast_to(alpha, (1, B))
        half_adjoint_products(blk, core, pick_half(pick_r[...], tb[it + 1, core]), prod, False)
        pltpu.make_async_copy(got, got, p_ssem).wait()
        done.wait()
        half_adjoint_products(blk, 1 - core, pick_half(pick_r[...], tb[it + 1, 1 - core]), prod, True)
        adjoint_place(lane_squares(tb[it + 1, 0]) + lane_squares(tb[it + 1, 1]))

    block_products(blk, pick_rows(pick_r[...], data[...]), prod, loads)
    adjoint_place(lane_squares(data[...]))
    pl.semaphore_wait(barrier, N_ROW + N_COL - 2)
    start_adjoint_send(0)
    tb[0, 0], tb[0, 1] = halves(data[...])

    def transpose_pair(n, carry):
        first = (n // 16) * 32 + (n % 2) * 16 + (n // 2) % 8
        for h in range(2):
            rows = slice(h * (B // 2), (h + 1) * (B // 2))
            blk_t[h, n] = jnp.concatenate([blk[first, rows], blk[first + 8, rows]], axis=0).T
        return carry

    lax.fori_loop(0, NB // 2, transpose_pair, 0, unroll=8)
    finish_adjoint(0, True)

    def step(it, carry):
        forward_and_adjoint(it)
        start_adjoint_send(it + 1)
        finish_adjoint(it + 1, False)
        return carry

    lax.fori_loop(0, ITERS, step, 0)

    alphas = [scal[i, 0:1, 0:1] for i in range(ITERS)]
    betas = [scal[i, 1:2, 0:1] for i in range(ITERS + 1)]
    top, bottom = whole(tb[ITERS, 0] / betas[ITERS], tb[ITERS, 1] / betas[ITERS])
    out[2, :HALF] = top
    out[2, HALF:] = bottom
    search = wb[0].reshape(NB, B) / alphas[0]
    answer = jnp.zeros((NB, B), F32)
    phibar, rhobar = betas[0], alphas[0]
    for i in range(ITERS):
        beta = betas[i + 1]
        rho = jnp.sqrt(rhobar * rhobar + beta * beta)
        cosine, sine = rhobar / rho, beta / rho
        phi = cosine * phibar
        phibar = sine * phibar
        answer = answer + (phi / rho) * search
        if i + 1 < ITERS:
            theta = sine * alphas[i + 1]
            rhobar = -cosine * alphas[i + 1]
            search = wb[i + 1].reshape(NB, B) / alphas[i + 1] - (theta / rho) * search
    out[0] = answer
    others = brecv.at[pl.ds(0, N_ROW - 1)]
    pltpu.make_async_copy(others, others, b_rsem).wait()
    alpha = norm_of(jnp.sum(brecv[...], axis=0))
    out[1] = wb[ITERS].reshape(NB, B) / alpha - (sine * alpha / rho) * search
    pltpu.make_async_copy(others, others, b_ssem).wait()


def per_device(blocks, block_rows, block_cols, counts, data):
    vec = jax.ShapeDtypeStruct((NB, B), F32)
    hbm = pl.BlockSpec(memory_space=pl.ANY)

    def in_hbm(a):
        return pltpu.with_memory_space_constraint(a, pltpu.HBM)

    out = pl.pallas_call(
        kernel,
        out_shape=jax.ShapeDtypeStruct((3, NB, B), F32),
        in_specs=[hbm, hbm, hbm, pl.BlockSpec(memory_space=pltpu.SMEM), hbm],
        out_specs=pl.BlockSpec(memory_space=pltpu.VMEM),
        scratch_shapes=[
            pltpu.VMEM((NB, B, B), BF16),
            pltpu.VMEM((2, NB // 2, B, B), BF16),
            pltpu.VMEM((1, NB), jnp.int32),
            pltpu.VMEM((1, NB), jnp.int32),
            pltpu.VMEM((NB, NB), BF16),
            pltpu.VMEM((NB, NB), BF16),
            pltpu.VMEM((NB, NB), BF16),
            pltpu.VMEM((NB, NB), BF16),
            pltpu.VMEM((NB, B), F32),
            pltpu.VMEM((NB, B), F32),
            pltpu.VMEM((ITERS + 1, 2, HALF, B), F32),
            pltpu.VMEM((ITERS + 1, N_ROW, RCH, B), F32),
            pltpu.VMEM((N_ROW, RCH + 1, B), F32),
            pltpu.VMEM((ITERS + 1, N_ROW, RCH + 1, B), F32),
            pltpu.VMEM((HALF + 1, B), F32),
            pltpu.VMEM((ITERS, HALF + 1, B), F32),
            pltpu.VMEM((HALF + 1, B), F32),
            pltpu.VMEM((ITERS, NY, HALF + 1, B), F32),
            pltpu.VMEM((1, B), F32),
            pltpu.VMEM((N_COL, 1, B), F32),
            pltpu.VMEM((1, B), F32),
            pltpu.VMEM((N_ROW, 1, B), F32),
            pltpu.VMEM((ITERS + 1, 8, B), F32),
            pltpu.SemaphoreType.DMA((3,)),
            pltpu.SemaphoreType.DMA((LOADS,)),
            pltpu.SemaphoreType.DMA,
            pltpu.SemaphoreType.DMA((ITERS + 1,)),
            pltpu.SemaphoreType.DMA,
            pltpu.SemaphoreType.DMA((ITERS + 1,)),
            pltpu.SemaphoreType.DMA,
            pltpu.SemaphoreType.DMA((ITERS,)),
            pltpu.SemaphoreType.DMA,
            pltpu.SemaphoreType.DMA((ITERS,)),
            pltpu.SemaphoreType.DMA,
            pltpu.SemaphoreType.DMA((ITERS,)),
            pltpu.SemaphoreType.DMA,
            pltpu.SemaphoreType.DMA,
            pltpu.SemaphoreType.DMA,
            pltpu.SemaphoreType.DMA,
        ],
        compiler_params=pltpu.CompilerParams(
            collective_id=0, has_side_effects=True, vmem_limit_bytes=53000 * 1024
        ),
        name="lsqr",
    )(blocks, in_hbm(block_rows[0]), in_hbm(block_cols[0]), counts, in_hbm(data.reshape(NB, B)))
    return out[0].reshape(-1), out[1].reshape(-1), out[2].reshape(-1)


def solution(mesh):
    return jax.shard_map(
        per_device,
        mesh=mesh,
        in_specs=(
            P("row", "col", None, None, None),
            P("row", "col", None),
            P("row", "col", None),
            P("row", "col"),
            P("row"),
        ),
        out_specs=(P("col"), P("col"), P("row")),
        check_vma=False,
    )
```

```python
import jax
import jax.numpy as jnp
from jax import lax
from jax.experimental import pallas as pl
from jax.experimental.pallas import tpu as pltpu
from jax.sharding import PartitionSpec as P

MESH = pl.DeviceIdType.MESH
F32 = jnp.float32
BF16 = jnp.bfloat16
EPS = 1e-06
ITERS = 3
B = 128
NB = 256
NX, NZ, NY, NC = 4, 8, 4, 2
N_ROW = NX * NZ
N_COL = NY * NC
RCH = NB // N_ROW
LOADS = 4
HALF = NB // NC
GROUP = 16
NEAR = NZ // 2
HALF_OWNERS = N_ROW // 2


def ring(step, size):
    return min(step, size - step)


ROW_STEPS = sorted(
    ((dx, dz) for dx in range(NX) for dz in range(NZ) if dx or dz),
    key=lambda s: -(ring(s[0], NX) + ring(s[1], NZ)),
)

COL_STEPS = sorted(
    ((dy, dc) for dy in range(NY) for dc in range(NC) if dy or dc),
    key=lambda s: -(2 * ring(s[0], NY) + s[1]),
)


def block_products(blocks_ref, picks, out_ref, loads=()):
    row = lax.broadcasted_iota(jnp.int32, (GROUP, B), 0)
    half = GROUP // 2
    for g in range(NB // GROUP):
        base = g * GROUP
        if loads and base % (NB // LOADS) == 0:
            loads[base * LOADS // NB].wait()
        mine = picks[base : base + GROUP]
        lhs = jnp.concatenate(
            [jnp.where((row & (half - 1)) == q, mine, 0.0).astype(BF16) for q in range(half)], axis=1
        )
        left = jnp.concatenate([blocks_ref[base + q] for q in range(half)], axis=0)
        right = jnp.concatenate([blocks_ref[base + half + q] for q in range(half)], axis=0)
        rhs = jnp.concatenate([left, right], axis=1)
        res = jnp.dot(lhs, rhs, preferred_element_type=F32)
        out_ref[base : base + GROUP, :] = jnp.where(row < half, res[:, :B], res[:, B:])


def swap_lanes(a):
    return jnp.concatenate([a[:, B // 2 :], a[:, : B // 2]], axis=1)


def left_lanes(rows):
    return lax.broadcasted_iota(jnp.int32, (rows, B), 1) < B // 2


def halves(vector):
    low, high = vector[:HALF], vector[HALF:]
    left = left_lanes(HALF)
    return jnp.where(left, low, swap_lanes(high)), jnp.where(left, swap_lanes(low), high)


def whole(first, second):
    left = left_lanes(HALF)
    return jnp.where(left, first, swap_lanes(second)), jnp.where(left, swap_lanes(first), second)


def pick_half(pick, packed):
    packed = packed.astype(BF16)
    low = jnp.dot(pick[:, :HALF], packed, preferred_element_type=F32)
    high = jnp.dot(pick[:, HALF:], packed, preferred_element_type=F32)
    mixed = jnp.where(left_lanes(NB), low, high)
    return mixed + swap_lanes(mixed)


def quarter_products(store, hn, hk, picks, out_ref, add):
    wide = 2 * GROUP
    row = lax.broadcasted_iota(jnp.int32, (wide, B), 0)
    side = jnp.where(left_lanes(wide), 0, 1)
    upper = lax.broadcasted_iota(jnp.int32, (GROUP, B), 0) < 8
    keep = (upper & left_lanes(GROUP)) | (~upper & ~left_lanes(GROUP))
    rows = pl.ds(pl.multiple_of(hk * (B // 2), B // 2), B // 2)
    for g in range(NB // wide):
        base = g * wide
        mine = picks[base : base + wide]
        lhs = jnp.concatenate(
            [jnp.where((row & 7) == q + side, mine, 0.0).astype(BF16) for q in range(0, 8, 2)], axis=1
        )
        left = jnp.concatenate([store[hn, (g * 8 + q) * 2, rows] for q in range(8)], axis=0)
        right = jnp.concatenate([store[hn, (g * 8 + q) * 2 + 1, rows] for q in range(8)], axis=0)
        res = jnp.dot(lhs, jnp.concatenate([left, right], axis=1), preferred_element_type=F32)
        low = jnp.where(keep, res[:GROUP, :B], 0.0)
        high = jnp.where(keep, res[GROUP:, B:], 0.0)
        if add:
            low = low + out_ref[base : base + GROUP, :]
            high = high + out_ref[base + GROUP : base + wide, :]
        out_ref[base : base + GROUP, :] = low
        out_ref[base + GROUP : base + wide, :] = high


def scatter_half(place, prod):
    both = scatter_rows(place, prod)
    both = both + swap_lanes(both)
    return jnp.where(left_lanes(HALF), both[:HALF], both[HALF:])


def pick_rows(pick, vector):
    return jnp.dot(pick, vector.astype(BF16), preferred_element_type=F32)


def scatter_rows(place, prod):
    high = prod.astype(BF16)
    low = (prod - high.astype(F32)).astype(BF16)
    return jnp.dot(place, high, preferred_element_type=F32) + jnp.dot(
        place, low, preferred_element_type=F32
    )


def lane_squares(vector):
    return jnp.sum(vector * vector, axis=0, keepdims=True)


def norm_of(parts):
    return jnp.sqrt(jnp.sum(parts, axis=(0, 1), keepdims=True) + EPS)


def kernel(
    blocks_hbm, rows_hbm, cols_hbm, counts_ref, data_hbm,
    out,
    blk, blk_t, blk_n, rows_v, cols_v, pick_r, pick_c, place_r, place_c, prod, prod_b,
    data, tb, wb, gsend, grecv, fsend, frecv, psend, precv, asend, arecv, bsend, brecv, scal,
    in_sem, blk_sem, g_ssem, g_rsem, w_ssem, w_rsem, f_ssem, f_rsem, p_ssem, p_rsem, t_ssem, t_rsem, a_ssem, a_rsem, b_ssem, b_rsem,
):
    r = lax.axis_index("row")
    c = lax.axis_index("col")
    x, z = r // NZ, r % NZ
    y, core = c // NC, c % NC
    row_xz = [((x + dx) % NX, (z + dz) % NZ) for dx, dz in ROW_STEPS]
    row_peers = [px * NZ + pz for px, pz in row_xz]
    near = z // NEAR
    steps = [(dx, dz) for dx in (2, 1, 3, 0) for dz in range(NEAR)]
    far_xz = [((x + dx) % NX, (1 - near) * NEAR + (z + dz) % NEAR) for dx, dz in steps]
    near_xz = [((x + dx) % NX, near * NEAR + (z + dz) % NEAR) for dx, dz in steps if dx or dz]

    def chunk_of(px, pz):
        return (pz // NEAR) * HALF_OWNERS + px * NEAR + pz % NEAR

    own = chunk_of(x, z)
    twin = y * NC + 1 - core
    y_peers = [((y + dy) % NY) * NC + core for dy in (2, 1, 3)]
    col_peers = [((y + dy) % NY) * NC + (core + dc) % NC for dy, dc in COL_STEPS]

    barrier = pltpu.get_barrier_semaphore()
    for p in row_peers:
        pl.semaphore_signal(barrier, inc=1, device_id=(p, c), device_id_type=MESH)
    for p in col_peers:
        pl.semaphore_signal(barrier, inc=1, device_id=(r, p), device_id_type=MESH)

    small = [
        pltpu.make_async_copy(rows_hbm, rows_v, in_sem.at[0]),
        pltpu.make_async_copy(cols_hbm, cols_v, in_sem.at[1]),
        pltpu.make_async_copy(data_hbm, data, in_sem.at[2]),
    ]
    for copy in small:
        copy.start()
    part = NB // LOADS
    loads = [
        pltpu.make_async_copy(
            blocks_hbm.at[0, 0, pl.ds(i * part, part)], blk.at[pl.ds(i * part, part)], blk_sem.at[i]
        )
        for i in range(LOADS)
    ]
    for copy in loads:
        copy.start()
    for copy in small:
        copy.wait()

    count = counts_ref[0, 0]
    sub = lax.broadcasted_iota(jnp.int32, (NB, NB), 0)
    lane = lax.broadcasted_iota(jnp.int32, (NB, NB), 1)
    live = lane < count

    def one_hot(index_ref):
        return (sub == index_ref[...]).astype(F32)

    hot_r = one_hot(rows_v)
    pick_r[...] = hot_r.T.astype(BF16)
    place_r[...] = jnp.where(live, hot_r, 0.0).astype(BF16)
    hot_c = one_hot(cols_v)
    pick_c[...] = hot_c.T.astype(BF16)
    place_c[...] = jnp.where(live, hot_c, 0.0).astype(BF16)

    def send_to_owners(it, owners):
        for px, pz in owners:
            pltpu.make_async_remote_copy(
                gsend.at[chunk_of(px, pz)], grecv.at[it, r], g_ssem, g_rsem.at[it],
                device_id=(px * NZ + pz, c), device_id_type=MESH,
            ).start()

    def put_squares(squares):
        gsend[:, RCH:, :] = jnp.broadcast_to(squares.reshape(1, 1, B), (N_ROW, 1, B))

    def put_half(h, packed):
        gsend[pl.ds(h * HALF_OWNERS, HALF_OWNERS), :RCH, :] = packed.reshape(HALF_OWNERS, RCH, B)

    def model_half(it, h):
        return wb[it, pl.ds(h * HALF_OWNERS, HALF_OWNERS)].reshape(HALF, B)

    def wait_chunks(it, which):
        landed = wb.at[it, pl.ds(0, HALF_OWNERS - 1 + which)]
        pltpu.make_async_copy(landed, landed, w_rsem.at[it, which]).wait()

    def wait_chunks_sent(it):
        sent = wb.at[it, pl.ds(0, N_ROW - 1)]
        pltpu.make_async_copy(sent, sent, w_ssem).wait()

    def start_last_norm():
        asend[...] = lane_squares(wb[ITERS, own])
        for p in col_peers:
            pltpu.make_async_remote_copy(
                asend, arecv.at[c], a_ssem, a_rsem, device_id=(r, p), device_id_type=MESH
            ).start()
        arecv[c] = asend[...]
        others = arecv.at[pl.ds(0, N_COL - 1)]
        pltpu.make_async_copy(others, others, a_rsem).wait()
        bsend[...] = jnp.sum(arecv[...], axis=0)
        for p in row_peers:
            pltpu.make_async_remote_copy(
                bsend, brecv.at[r], b_ssem, b_rsem, device_id=(p, c), device_id_type=MESH
            ).start()
        brecv[r] = bsend[...]
        pltpu.make_async_copy(others, others, a_ssem).wait()

    def finish_adjoint(it, first):
        before = None if first else wb[it - 1, own] / scal[it - 1, 0:1, 0:1]
        got = grecv.at[it, pl.ds(0, N_ROW - 1)]
        pltpu.make_async_copy(got, got, g_rsem.at[it]).wait()
        total = jnp.sum(grecv[it], axis=0)
        beta = norm_of(total[RCH:])
        chunk = total[:RCH] / beta
        if not first:
            chunk = chunk - beta * before
        wb[it, own] = chunk
        scal[it, 1:2, :] = jnp.broadcast_to(beta, (1, B))
        for px, pz in row_xz:
            pltpu.make_async_remote_copy(
                wb.at[it, own], wb.at[it, own], w_ssem, w_rsem.at[it, (pz // NEAR + near) % 2],
                device_id=(px * NZ + pz, c), device_id_type=MESH,
            ).start()
        if not first:
            pl.when(it == ITERS)(start_last_norm)
        pltpu.make_async_copy(got, got, g_ssem).wait()

    def forward_and_adjoint(it):
        wait_chunks(it, 0)
        part = model_half(it, near)
        picks = pick_half(pick_c[...], part)
        quarter_products(blk_t, 1 - core, near, picks, prod, False)
        quarter_products(blk_t, core, near, picks, prod_b, False)
        squares = lane_squares(part)
        wait_chunks(it, 1)
        part = model_half(it, 1 - near)
        picks = pick_half(pick_c[...], part)
        quarter_products(blk_t, 1 - core, 1 - near, picks, prod, True)
        both = lane_squares(part)
        squares = jnp.where(near == 0, squares, both) + jnp.where(near == 0, both, squares)
        fsend[:HALF, :] = scatter_half(place_r[...], prod[...])
        fsend[HALF:, :] = squares
        pair = pltpu.make_async_remote_copy(
            fsend, frecv.at[it], f_ssem, f_rsem.at[it], device_id=(r, twin), device_id_type=MESH
        )
        pair.start()
        quarter_products(blk_t, core, 1 - near, picks, prod_b, True)
        psend[:HALF, :] = scatter_half(place_r[...], prod_b[...])
        psend[HALF:, :] = squares
        pair.wait()
        psend[...] = psend[...] + frecv[it]
        for p in y_peers:
            pltpu.make_async_remote_copy(
                psend, precv.at[it, y], p_ssem, p_rsem.at[it], device_id=(r, p), device_id_type=MESH
            ).start()
        precv[it, y] = psend[...]
        unit = tb[it, core] / scal[it, 1:2, 0:1]
        got = precv.at[it, pl.ds(0, NY - 1)]
        pltpu.make_async_copy(got, got, p_rsem.at[it]).wait()
        total = jnp.sum(precv[it], axis=0)
        alpha = norm_of(total[HALF:])
        tb[it + 1, core] = total[:HALF] / alpha - alpha * unit
        done = pltpu.make_async_remote_copy(
            tb.at[it + 1, core], tb.at[it + 1, core], t_ssem, t_rsem.at[it],
            device_id=(r, twin), device_id_type=MESH,
        )
        done.start()
        scal[it, 0:1, :] = jnp.broadcast_to(alpha, (1, B))
        picks = pick_half(pick_r[...], tb[it + 1, core])
        quarter_products(blk_n, 1 - near, core, picks, prod, False)
        quarter_products(blk_n, near, core, picks, prod_b, False)
        pltpu.make_async_copy(got, got, p_ssem).wait()
        wait_chunks_sent(it)
        done.wait()
        picks = pick_half(pick_r[...], tb[it + 1, 1 - core])
        quarter_products(blk_n, 1 - near, 1 - core, picks, prod, True)
        put_squares(lane_squares(tb[it + 1, 0]) + lane_squares(tb[it + 1, 1]))
        put_half(1 - near, scatter_half(place_c[...], prod[...]))
        send_to_owners(it + 1, far_xz)
        quarter_products(blk_n, near, 1 - core, picks, prod_b, True)
        put_half(near, scatter_half(place_c[...], prod_b[...]))
        send_to_owners(it + 1, near_xz)
        grecv[it + 1, r] = gsend[own]

    block_products(blk, pick_rows(pick_r[...], data[...]), prod, loads)
    first, second = halves(scatter_rows(place_c[...], prod[...]))
    put_half(0, first)
    put_half(1, second)
    put_squares(lane_squares(data[...]))
    pl.semaphore_wait(barrier, N_ROW + N_COL - 2)
    send_to_owners(0, row_xz)
    grecv[0, r] = gsend[own]
    tb[0, 0], tb[0, 1] = halves(data[...])

    def pair_of(n):
        return (n // 16) * 32 + (n % 2) * 16 + (n // 2) % 8

    def transpose_pair(n, carry):
        k = pair_of(n)
        for h in range(2):
            rows = slice(h * (B // 2), (h + 1) * (B // 2))
            blk_t[h, n] = jnp.concatenate([blk[k, rows], blk[k + 8, rows]], axis=0).T
        return carry

    def repack_pair(n, carry):
        k = pair_of(n)
        one, two = blk[k], blk[k + 8]
        half = B // 2
        blk_n[0, n] = jnp.concatenate([one[:, :half], two[:, :half]], axis=1)
        blk_n[1, n] = jnp.concatenate([one[:, half:], two[:, half:]], axis=1)
        return carry

    lax.fori_loop(0, NB // 2, transpose_pair, 0, unroll=8)
    finish_adjoint(0, True)
    lax.fori_loop(0, NB // 2, repack_pair, 0, unroll=8)

    def step(it, carry):
        forward_and_adjoint(it)
        finish_adjoint(it + 1, False)
        return carry

    lax.fori_loop(0, ITERS, step, 0)

    alphas = [scal[i, 0:1, 0:1] for i in range(ITERS)]
    betas = [scal[i, 1:2, 0:1] for i in range(ITERS + 1)]
    top, bottom = whole(tb[ITERS, 0] / betas[ITERS], tb[ITERS, 1] / betas[ITERS])
    out[2, :HALF] = top
    out[2, HALF:] = bottom
    wait_chunks(ITERS, 0)
    wait_chunks(ITERS, 1)
    wait_chunks_sent(ITERS)
    search = wb[0].reshape(NB, B) / alphas[0]
    answer = jnp.zeros((NB, B), F32)
    phibar, rhobar = betas[0], alphas[0]
    for i in range(ITERS):
        beta = betas[i + 1]
        rho = jnp.sqrt(rhobar * rhobar + beta * beta)
        cosine, sine = rhobar / rho, beta / rho
        phi = cosine * phibar
        phibar = sine * phibar
        answer = answer + (phi / rho) * search
        if i + 1 < ITERS:
            theta = sine * alphas[i + 1]
            rhobar = -cosine * alphas[i + 1]
            search = wb[i + 1].reshape(NB, B) / alphas[i + 1] - (theta / rho) * search
    top, bottom = whole(answer[:HALF], answer[HALF:])
    out[0, :HALF] = top
    out[0, HALF:] = bottom
    others = brecv.at[pl.ds(0, N_ROW - 1)]
    pltpu.make_async_copy(others, others, b_rsem).wait()
    alpha = norm_of(jnp.sum(brecv[...], axis=0))
    search = wb[ITERS].reshape(NB, B) / alpha - (sine * alpha / rho) * search
    top, bottom = whole(search[:HALF], search[HALF:])
    out[1, :HALF] = top
    out[1, HALF:] = bottom
    pltpu.make_async_copy(others, others, b_ssem).wait()


def per_device(blocks, block_rows, block_cols, counts, data):
    vec = jax.ShapeDtypeStruct((NB, B), F32)
    hbm = pl.BlockSpec(memory_space=pl.ANY)

    def in_hbm(a):
        return pltpu.with_memory_space_constraint(a, pltpu.HBM)

    out = pl.pallas_call(
        kernel,
        out_shape=jax.ShapeDtypeStruct((3, NB, B), F32),
        in_specs=[hbm, hbm, hbm, pl.BlockSpec(memory_space=pltpu.SMEM), hbm],
        out_specs=pl.BlockSpec(memory_space=pltpu.VMEM),
        scratch_shapes=[
            pltpu.VMEM((NB, B, B), BF16),
            pltpu.VMEM((2, NB // 2, B, B), BF16),
            pltpu.VMEM((2, NB // 2, B, B), BF16),
            pltpu.VMEM((1, NB), jnp.int32),
            pltpu.VMEM((1, NB), jnp.int32),
            pltpu.VMEM((NB, NB), BF16),
            pltpu.VMEM((NB, NB), BF16),
            pltpu.VMEM((NB, NB), BF16),
            pltpu.VMEM((NB, NB), BF16),
            pltpu.VMEM((NB, B), F32),
            pltpu.VMEM((NB, B), F32),
            pltpu.VMEM((NB, B), F32),
            pltpu.VMEM((ITERS + 1, 2, HALF, B), F32),
            pltpu.VMEM((ITERS + 1, N_ROW, RCH, B), F32),
            pltpu.VMEM((N_ROW, RCH + 1, B), F32),
            pltpu.VMEM((ITERS + 1, N_ROW, RCH + 1, B), F32),
            pltpu.VMEM((HALF + 1, B), F32),
            pltpu.VMEM((ITERS, HALF + 1, B), F32),
            pltpu.VMEM((HALF + 1, B), F32),
            pltpu.VMEM((ITERS, NY, HALF + 1, B), F32),
            pltpu.VMEM((1, B), F32),
            pltpu.VMEM((N_COL, 1, B), F32),
            pltpu.VMEM((1, B), F32),
            pltpu.VMEM((N_ROW, 1, B), F32),
            pltpu.VMEM((ITERS + 1, 8, B), F32),
            pltpu.SemaphoreType.DMA((3,)),
            pltpu.SemaphoreType.DMA((LOADS,)),
            pltpu.SemaphoreType.DMA,
            pltpu.SemaphoreType.DMA((ITERS + 1,)),
            pltpu.SemaphoreType.DMA,
            pltpu.SemaphoreType.DMA((ITERS + 1, 2)),
            pltpu.SemaphoreType.DMA,
            pltpu.SemaphoreType.DMA((ITERS,)),
            pltpu.SemaphoreType.DMA,
            pltpu.SemaphoreType.DMA((ITERS,)),
            pltpu.SemaphoreType.DMA,
            pltpu.SemaphoreType.DMA((ITERS,)),
            pltpu.SemaphoreType.DMA,
            pltpu.SemaphoreType.DMA,
            pltpu.SemaphoreType.DMA,
            pltpu.SemaphoreType.DMA,
        ],
        compiler_params=pltpu.CompilerParams(
            collective_id=0, has_side_effects=True, vmem_limit_bytes=53000 * 1024
        ),
        name="lsqr",
    )(blocks, in_hbm(block_rows[0]), in_hbm(block_cols[0]), counts, in_hbm(data.reshape(NB, B)))
    return out[0].reshape(-1), out[1].reshape(-1), out[2].reshape(-1)


def solution(mesh):
    return jax.shard_map(
        per_device,
        mesh=mesh,
        in_specs=(
            P("row", "col", None, None, None),
            P("row", "col", None),
            P("row", "col", None),
            P("row", "col"),
            P("row"),
        ),
        out_specs=(P("col"), P("col"), P("row")),
        check_vma=False,
    )
```

```python
import jax
import jax.numpy as jnp
from jax import lax
from jax.experimental import pallas as pl
from jax.experimental.pallas import tpu as pltpu
from jax.sharding import PartitionSpec as P

MESH = pl.DeviceIdType.MESH
F32 = jnp.float32
BF16 = jnp.bfloat16
EPS = 1e-06
ITERS = 3
B = 128
NB = 256
NX, NZ, NY, NC = 4, 8, 4, 2
N_ROW = NX * NZ
N_COL = NY * NC
RCH = NB // N_ROW
LOADS = 4
HALF = NB // NC
GROUP = 16
NEAR = NZ // 2
HALF_OWNERS = N_ROW // 2


def ring(step, size):
    return min(step, size - step)


ROW_STEPS = sorted(
    ((dx, dz) for dx in range(NX) for dz in range(NZ) if dx or dz),
    key=lambda s: -(ring(s[0], NX) + ring(s[1], NZ)),
)

COL_STEPS = sorted(
    ((dy, dc) for dy in range(NY) for dc in range(NC) if dy or dc),
    key=lambda s: -(2 * ring(s[0], NY) + s[1]),
)


def block_products(blocks_ref, picks, out_ref, loads=()):
    row = lax.broadcasted_iota(jnp.int32, (GROUP, B), 0)
    half = GROUP // 2
    for g in range(NB // GROUP):
        base = g * GROUP
        if loads and base % (NB // LOADS) == 0:
            loads[base * LOADS // NB].wait()
        mine = picks[base : base + GROUP]
        lhs = jnp.concatenate(
            [jnp.where((row & (half - 1)) == q, mine, 0.0).astype(BF16) for q in range(half)], axis=1
        )
        left = jnp.concatenate([blocks_ref[base + q] for q in range(half)], axis=0)
        right = jnp.concatenate([blocks_ref[base + half + q] for q in range(half)], axis=0)
        rhs = jnp.concatenate([left, right], axis=1)
        res = jnp.dot(lhs, rhs, preferred_element_type=F32)
        out_ref[base : base + GROUP, :] = jnp.where(row < half, res[:, :B], res[:, B:])


def swap_lanes(a):
    return jnp.concatenate([a[:, B // 2 :], a[:, : B // 2]], axis=1)


def left_lanes(rows):
    return lax.broadcasted_iota(jnp.int32, (rows, B), 1) < B // 2


def halves(vector):
    low, high = vector[:HALF], vector[HALF:]
    left = left_lanes(HALF)
    return jnp.where(left, low, swap_lanes(high)), jnp.where(left, swap_lanes(low), high)


def whole(first, second):
    left = left_lanes(HALF)
    return jnp.where(left, first, swap_lanes(second)), jnp.where(left, swap_lanes(first), second)


def pick_half(pick, packed):
    packed = packed.astype(BF16)
    low = jnp.dot(pick[:, :HALF], packed, preferred_element_type=F32)
    high = jnp.dot(pick[:, HALF:], packed, preferred_element_type=F32)
    mixed = jnp.where(left_lanes(NB), low, high)
    return mixed + swap_lanes(mixed)


def half_adjoint_products(blocks_ref, h, picks, out_ref, add):
    row = lax.broadcasted_iota(jnp.int32, (GROUP, B), 0)
    side = jnp.where(left_lanes(GROUP), 0, 1)
    half = GROUP // 2
    rows = pl.ds(pl.multiple_of(h * (B // 2), B // 2), B // 2)
    for g in range(NB // GROUP):
        base = g * GROUP
        mine = picks[base : base + GROUP]
        lhs = jnp.concatenate(
            [jnp.where((row & (half - 1)) == q + side, mine, 0.0).astype(BF16) for q in range(0, half, 2)], axis=1
        )
        left = jnp.concatenate([blocks_ref[base + q, rows] for q in range(half)], axis=0)
        right = jnp.concatenate([blocks_ref[base + half + q, rows] for q in range(half)], axis=0)
        res = jnp.dot(lhs, jnp.concatenate([left, right], axis=1), preferred_element_type=F32)
        res = jnp.where(row < half, res[:, :B], res[:, B:])
        if add:
            res = res + out_ref[base : base + GROUP, :]
        out_ref[base : base + GROUP, :] = res


def quarter_products(store, hn, hk, picks, out_ref, add):
    wide = 2 * GROUP
    row = lax.broadcasted_iota(jnp.int32, (wide, B), 0)
    side = jnp.where(left_lanes(wide), 0, 1)
    upper = lax.broadcasted_iota(jnp.int32, (GROUP, B), 0) < 8
    keep = (upper & left_lanes(GROUP)) | (~upper & ~left_lanes(GROUP))
    rows = pl.ds(pl.multiple_of(hk * (B // 2), B // 2), B // 2)
    for g in range(NB // wide):
        base = g * wide
        mine = picks[base : base + wide]
        lhs = jnp.concatenate(
            [jnp.where((row & 7) == q + side, mine, 0.0).astype(BF16) for q in range(0, 8, 2)], axis=1
        )
        left = jnp.concatenate([store[hn, (g * 8 + q) * 2, rows] for q in range(8)], axis=0)
        right = jnp.concatenate([store[hn, (g * 8 + q) * 2 + 1, rows] for q in range(8)], axis=0)
        res = jnp.dot(lhs, jnp.concatenate([left, right], axis=1), preferred_element_type=F32)
        low = jnp.where(keep, res[:GROUP, :B], 0.0)
        high = jnp.where(keep, res[GROUP:, B:], 0.0)
        if add:
            low = low + out_ref[base : base + GROUP, :]
            high = high + out_ref[base + GROUP : base + wide, :]
        out_ref[base : base + GROUP, :] = low
        out_ref[base + GROUP : base + wide, :] = high


def scatter_half(place, prod):
    both = scatter_rows(place, prod)
    both = both + swap_lanes(both)
    return jnp.where(left_lanes(HALF), both[:HALF], both[HALF:])


def pick_rows(pick, vector):
    return jnp.dot(pick, vector.astype(BF16), preferred_element_type=F32)


def scatter_rows(place, prod):
    high = prod.astype(BF16)
    low = (prod - high.astype(F32)).astype(BF16)
    return jnp.dot(place, high, preferred_element_type=F32) + jnp.dot(
        place, low, preferred_element_type=F32
    )


def lane_squares(vector):
    return jnp.sum(vector * vector, axis=0, keepdims=True)


def norm_of(parts):
    return jnp.sqrt(jnp.sum(parts, axis=(0, 1), keepdims=True) + EPS)


def kernel(
    blocks_hbm, rows_hbm, cols_hbm, counts_ref, data_hbm,
    out,
    blk, blk_t, rows_v, cols_v, pick_r, pick_c, place_r, place_c, prod, prod_b,
    data, tb, wb, gsend, grecv, fsend, frecv, psend, precv, asend, arecv, bsend, brecv, scal,
    in_sem, blk_sem, g_ssem, g_rsem, w_ssem, w_rsem, f_ssem, f_rsem, p_ssem, p_rsem, t_ssem, t_rsem, a_ssem, a_rsem, b_ssem, b_rsem,
):
    r = lax.axis_index("row")
    c = lax.axis_index("col")
    x, z = r // NZ, r % NZ
    y, core = c // NC, c % NC
    row_xz = [((x + dx) % NX, (z + dz) % NZ) for dx, dz in ROW_STEPS]
    row_peers = [px * NZ + pz for px, pz in row_xz]
    near = z // NEAR

    def chunk_of(px, pz):
        return (pz // NEAR) * HALF_OWNERS + px * NEAR + pz % NEAR

    own = chunk_of(x, z)
    twin = y * NC + 1 - core
    y_peers = [((y + dy) % NY) * NC + core for dy in (2, 1, 3)]
    col_peers = [((y + dy) % NY) * NC + (core + dc) % NC for dy, dc in COL_STEPS]

    barrier = pltpu.get_barrier_semaphore()
    for p in row_peers:
        pl.semaphore_signal(barrier, inc=1, device_id=(p, c), device_id_type=MESH)
    for p in col_peers:
        pl.semaphore_signal(barrier, inc=1, device_id=(r, p), device_id_type=MESH)

    small = [
        pltpu.make_async_copy(rows_hbm, rows_v, in_sem.at[0]),
        pltpu.make_async_copy(cols_hbm, cols_v, in_sem.at[1]),
        pltpu.make_async_copy(data_hbm, data, in_sem.at[2]),
    ]
    for copy in small:
        copy.start()
    part = NB // LOADS
    loads = [
        pltpu.make_async_copy(
            blocks_hbm.at[0, 0, pl.ds(i * part, part)], blk.at[pl.ds(i * part, part)], blk_sem.at[i]
        )
        for i in range(LOADS)
    ]
    for copy in loads:
        copy.start()
    for copy in small:
        copy.wait()

    count = counts_ref[0, 0]
    sub = lax.broadcasted_iota(jnp.int32, (NB, NB), 0)
    lane = lax.broadcasted_iota(jnp.int32, (NB, NB), 1)
    live = lane < count

    def one_hot(index_ref):
        return (sub == index_ref[...]).astype(F32)

    hot_r = one_hot(rows_v)
    pick_r[...] = hot_r.T.astype(BF16)
    place_r[...] = jnp.where(live, hot_r, 0.0).astype(BF16)
    hot_c = one_hot(cols_v)
    pick_c[...] = hot_c.T.astype(BF16)
    place_c[...] = jnp.where(live, hot_c, 0.0).astype(BF16)

    def put_parts(squares):
        parts = halves(scatter_rows(place_c[...], prod[...]))
        for h in range(2):
            gsend[h * HALF_OWNERS : (h + 1) * HALF_OWNERS, :RCH, :] = parts[h].reshape(HALF_OWNERS, RCH, B)
        gsend[:, RCH:, :] = jnp.broadcast_to(squares.reshape(1, 1, B), (N_ROW, 1, B))

    def send_to_owners(it):
        for px, pz in row_xz:
            pltpu.make_async_remote_copy(
                gsend.at[chunk_of(px, pz)], grecv.at[it, r], g_ssem, g_rsem.at[it],
                device_id=(px * NZ + pz, c), device_id_type=MESH,
            ).start()
        grecv[it, r] = gsend[own]

    def model_half(it, h):
        return wb[it, pl.ds(h * HALF_OWNERS, HALF_OWNERS)].reshape(HALF, B)

    def wait_chunks(it, which):
        landed = wb.at[it, pl.ds(0, HALF_OWNERS - 1 + which)]
        pltpu.make_async_copy(landed, landed, w_rsem.at[it, which]).wait()

    def wait_chunks_sent(it):
        sent = wb.at[it, pl.ds(0, N_ROW - 1)]
        pltpu.make_async_copy(sent, sent, w_ssem).wait()

    def start_last_norm():
        asend[...] = lane_squares(wb[ITERS, own])
        for p in col_peers:
            pltpu.make_async_remote_copy(
                asend, arecv.at[c], a_ssem, a_rsem, device_id=(r, p), device_id_type=MESH
            ).start()
        arecv[c] = asend[...]
        others = arecv.at[pl.ds(0, N_COL - 1)]
        pltpu.make_async_copy(others, others, a_rsem).wait()
        bsend[...] = jnp.sum(arecv[...], axis=0)
        for p in row_peers:
            pltpu.make_async_remote_copy(
                bsend, brecv.at[r], b_ssem, b_rsem, device_id=(p, c), device_id_type=MESH
            ).start()
        brecv[r] = bsend[...]
        pltpu.make_async_copy(others, others, a_ssem).wait()

    def finish_adjoint(it, first):
        before = None if first else wb[it - 1, own] / scal[it - 1, 0:1, 0:1]
        got = grecv.at[it, pl.ds(0, N_ROW - 1)]
        pltpu.make_async_copy(got, got, g_rsem.at[it]).wait()
        total = jnp.sum(grecv[it], axis=0)
        beta = norm_of(total[RCH:])
        chunk = total[:RCH] / beta
        if not first:
            chunk = chunk - beta * before
        wb[it, own] = chunk
        scal[it, 1:2, :] = jnp.broadcast_to(beta, (1, B))
        for px, pz in row_xz:
            pltpu.make_async_remote_copy(
                wb.at[it, own], wb.at[it, own], w_ssem, w_rsem.at[it, (pz // NEAR + near) % 2],
                device_id=(px * NZ + pz, c), device_id_type=MESH,
            ).start()
        if not first:
            pl.when(it == ITERS)(start_last_norm)
        pltpu.make_async_copy(got, got, g_ssem).wait()

    def forward_and_adjoint(it):
        wait_chunks(it, 0)
        part = model_half(it, near)
        picks = pick_half(pick_c[...], part)
        quarter_products(blk_t, 1 - core, near, picks, prod, False)
        quarter_products(blk_t, core, near, picks, prod_b, False)
        squares = lane_squares(part)
        wait_chunks(it, 1)
        part = model_half(it, 1 - near)
        picks = pick_half(pick_c[...], part)
        quarter_products(blk_t, 1 - core, 1 - near, picks, prod, True)
        both = lane_squares(part)
        squares = jnp.where(near == 0, squares, both) + jnp.where(near == 0, both, squares)
        fsend[:HALF, :] = scatter_half(place_r[...], prod[...])
        fsend[HALF:, :] = squares
        pair = pltpu.make_async_remote_copy(
            fsend, frecv.at[it], f_ssem, f_rsem.at[it], device_id=(r, twin), device_id_type=MESH
        )
        pair.start()
        quarter_products(blk_t, core, 1 - near, picks, prod_b, True)
        psend[:HALF, :] = scatter_half(place_r[...], prod_b[...])
        psend[HALF:, :] = squares
        pair.wait()
        psend[...] = psend[...] + frecv[it]
        for p in y_peers:
            pltpu.make_async_remote_copy(
                psend, precv.at[it, y], p_ssem, p_rsem.at[it], device_id=(r, p), device_id_type=MESH
            ).start()
        precv[it, y] = psend[...]
        unit = tb[it, core] / scal[it, 1:2, 0:1]
        got = precv.at[it, pl.ds(0, NY - 1)]
        pltpu.make_async_copy(got, got, p_rsem.at[it]).wait()
        total = jnp.sum(precv[it], axis=0)
        alpha = norm_of(total[HALF:])
        tb[it + 1, core] = total[:HALF] / alpha - alpha * unit
        done = pltpu.make_async_remote_copy(
            tb.at[it + 1, core], tb.at[it + 1, core], t_ssem, t_rsem.at[it],
            device_id=(r, twin), device_id_type=MESH,
        )
        done.start()
        scal[it, 0:1, :] = jnp.broadcast_to(alpha, (1, B))
        picks = pick_half(pick_r[...], tb[it + 1, core])
        half_adjoint_products(blk, core, picks, prod, False)
        pltpu.make_async_copy(got, got, p_ssem).wait()
        wait_chunks_sent(it)
        squares = lane_squares(tb[it + 1, core])
        done.wait()
        other = tb[it + 1, 1 - core]
        half_adjoint_products(blk, 1 - core, pick_half(pick_r[...], other), prod, True)
        both = lane_squares(other)
        put_parts(jnp.where(core == 0, squares, both) + jnp.where(core == 0, both, squares))
        send_to_owners(it + 1)

    block_products(blk, pick_rows(pick_r[...], data[...]), prod, loads)
    put_parts(lane_squares(data[...]))
    pl.semaphore_wait(barrier, N_ROW + N_COL - 2)
    send_to_owners(0)
    tb[0, 0], tb[0, 1] = halves(data[...])

    def pair_of(n):
        return (n // 16) * 32 + (n % 2) * 16 + (n // 2) % 8

    def transpose_pair(n, carry):
        k = pair_of(n)
        for h in range(2):
            rows = slice(h * (B // 2), (h + 1) * (B // 2))
            blk_t[h, n] = jnp.concatenate([blk[k, rows], blk[k + 8, rows]], axis=0).T
        return carry

    lax.fori_loop(0, NB // 2, transpose_pair, 0, unroll=8)
    finish_adjoint(0, True)

    def step(it, carry):
        forward_and_adjoint(it)
        finish_adjoint(it + 1, False)
        return carry

    lax.fori_loop(0, ITERS, step, 0)

    alphas = [scal[i, 0:1, 0:1] for i in range(ITERS)]
    betas = [scal[i, 1:2, 0:1] for i in range(ITERS + 1)]
    top, bottom = whole(tb[ITERS, 0] / betas[ITERS], tb[ITERS, 1] / betas[ITERS])
    out[2, :HALF] = top
    out[2, HALF:] = bottom
    wait_chunks(ITERS, 0)
    wait_chunks(ITERS, 1)
    wait_chunks_sent(ITERS)
    search = wb[0].reshape(NB, B) / alphas[0]
    answer = jnp.zeros((NB, B), F32)
    phibar, rhobar = betas[0], alphas[0]
    for i in range(ITERS):
        beta = betas[i + 1]
        rho = jnp.sqrt(rhobar * rhobar + beta * beta)
        cosine, sine = rhobar / rho, beta / rho
        phi = cosine * phibar
        phibar = sine * phibar
        answer = answer + (phi / rho) * search
        if i + 1 < ITERS:
            theta = sine * alphas[i + 1]
            rhobar = -cosine * alphas[i + 1]
            search = wb[i + 1].reshape(NB, B) / alphas[i + 1] - (theta / rho) * search
    top, bottom = whole(answer[:HALF], answer[HALF:])
    out[0, :HALF] = top
    out[0, HALF:] = bottom
    others = brecv.at[pl.ds(0, N_ROW - 1)]
    pltpu.make_async_copy(others, others, b_rsem).wait()
    alpha = norm_of(jnp.sum(brecv[...], axis=0))
    search = wb[ITERS].reshape(NB, B) / alpha - (sine * alpha / rho) * search
    top, bottom = whole(search[:HALF], search[HALF:])
    out[1, :HALF] = top
    out[1, HALF:] = bottom
    pltpu.make_async_copy(others, others, b_ssem).wait()


def per_device(blocks, block_rows, block_cols, counts, data):
    vec = jax.ShapeDtypeStruct((NB, B), F32)
    hbm = pl.BlockSpec(memory_space=pl.ANY)

    def in_hbm(a):
        return pltpu.with_memory_space_constraint(a, pltpu.HBM)

    out = pl.pallas_call(
        kernel,
        out_shape=jax.ShapeDtypeStruct((3, NB, B), F32),
        in_specs=[hbm, hbm, hbm, pl.BlockSpec(memory_space=pltpu.SMEM), hbm],
        out_specs=pl.BlockSpec(memory_space=pltpu.VMEM),
        scratch_shapes=[
            pltpu.VMEM((NB, B, B), BF16),
            pltpu.VMEM((2, NB // 2, B, B), BF16),
            pltpu.VMEM((1, NB), jnp.int32),
            pltpu.VMEM((1, NB), jnp.int32),
            pltpu.VMEM((NB, NB), BF16),
            pltpu.VMEM((NB, NB), BF16),
            pltpu.VMEM((NB, NB), BF16),
            pltpu.VMEM((NB, NB), BF16),
            pltpu.VMEM((NB, B), F32),
            pltpu.VMEM((NB, B), F32),
            pltpu.VMEM((NB, B), F32),
            pltpu.VMEM((ITERS + 1, 2, HALF, B), F32),
            pltpu.VMEM((ITERS + 1, N_ROW, RCH, B), F32),
            pltpu.VMEM((N_ROW, RCH + 1, B), F32),
            pltpu.VMEM((ITERS + 1, N_ROW, RCH + 1, B), F32),
            pltpu.VMEM((HALF + 1, B), F32),
            pltpu.VMEM((ITERS, HALF + 1, B), F32),
            pltpu.VMEM((HALF + 1, B), F32),
            pltpu.VMEM((ITERS, NY, HALF + 1, B), F32),
            pltpu.VMEM((1, B), F32),
            pltpu.VMEM((N_COL, 1, B), F32),
            pltpu.VMEM((1, B), F32),
            pltpu.VMEM((N_ROW, 1, B), F32),
            pltpu.VMEM((ITERS + 1, 8, B), F32),
            pltpu.SemaphoreType.DMA((3,)),
            pltpu.SemaphoreType.DMA((LOADS,)),
            pltpu.SemaphoreType.DMA,
            pltpu.SemaphoreType.DMA((ITERS + 1,)),
            pltpu.SemaphoreType.DMA,
            pltpu.SemaphoreType.DMA((ITERS + 1, 2)),
            pltpu.SemaphoreType.DMA,
            pltpu.SemaphoreType.DMA((ITERS,)),
            pltpu.SemaphoreType.DMA,
            pltpu.SemaphoreType.DMA((ITERS,)),
            pltpu.SemaphoreType.DMA,
            pltpu.SemaphoreType.DMA((ITERS,)),
            pltpu.SemaphoreType.DMA,
            pltpu.SemaphoreType.DMA,
            pltpu.SemaphoreType.DMA,
            pltpu.SemaphoreType.DMA,
        ],
        compiler_params=pltpu.CompilerParams(
            collective_id=0, has_side_effects=True, vmem_limit_bytes=53000 * 1024
        ),
        name="lsqr",
    )(blocks, in_hbm(block_rows[0]), in_hbm(block_cols[0]), counts, in_hbm(data.reshape(NB, B)))
    return out[0].reshape(-1), out[1].reshape(-1), out[2].reshape(-1)


def solution(mesh):
    return jax.shard_map(
        per_device,
        mesh=mesh,
        in_specs=(
            P("row", "col", None, None, None),
            P("row", "col", None),
            P("row", "col", None),
            P("row", "col"),
            P("row"),
        ),
        out_specs=(P("col"), P("col"), P("row")),
        check_vma=False,
    )
```

```python
import jax
import jax.numpy as jnp
from jax import lax
from jax.experimental import pallas as pl
from jax.experimental.pallas import tpu as pltpu
from jax.sharding import PartitionSpec as P

MESH = pl.DeviceIdType.MESH
F32 = jnp.float32
BF16 = jnp.bfloat16
EPS = 1e-06
ITERS = 3
B = 128
NB = 256
NX, NZ, NY, NC = 4, 8, 4, 2
N_ROW = NX * NZ
N_COL = NY * NC
RCH = NB // N_ROW
LOADS = 4
HALF = NB // NC
GROUP = 16


def ring(step, size):
    return min(step, size - step)


ROW_STEPS = sorted(
    ((dx, dz) for dx in range(NX) for dz in range(NZ) if dx or dz),
    key=lambda s: (-(ring(s[0], NX) + ring(s[1], NZ)), s[1], s[0]),
)

COL_STEPS = sorted(
    ((dy, dc) for dy in range(NY) for dc in range(NC) if dy or dc),
    key=lambda s: -(2 * ring(s[0], NY) + s[1]),
)


def block_products(blocks_ref, picks, out_ref, loads=()):
    row = lax.broadcasted_iota(jnp.int32, (GROUP, B), 0)
    half = GROUP // 2
    for g in range(NB // GROUP):
        base = g * GROUP
        if loads and base % (NB // LOADS) == 0:
            loads[base * LOADS // NB].wait()
        mine = picks[base : base + GROUP]
        lhs = jnp.concatenate(
            [jnp.where((row & (half - 1)) == q, mine, 0.0).astype(BF16) for q in range(half)], axis=1
        )
        left = jnp.concatenate([blocks_ref[base + q] for q in range(half)], axis=0)
        right = jnp.concatenate([blocks_ref[base + half + q] for q in range(half)], axis=0)
        rhs = jnp.concatenate([left, right], axis=1)
        res = jnp.dot(lhs, rhs, preferred_element_type=F32)
        out_ref[base : base + GROUP, :] = jnp.where(row < half, res[:, :B], res[:, B:])


def swap_lanes(a):
    return jnp.concatenate([a[:, B // 2 :], a[:, : B // 2]], axis=1)


def left_lanes(rows):
    return lax.broadcasted_iota(jnp.int32, (rows, B), 1) < B // 2


def halves(vector):
    low, high = vector[:HALF], vector[HALF:]
    left = left_lanes(HALF)
    return jnp.where(left, low, swap_lanes(high)), jnp.where(left, swap_lanes(low), high)


def whole(first, second):
    left = left_lanes(HALF)
    return jnp.where(left, first, swap_lanes(second)), jnp.where(left, swap_lanes(first), second)


def pick_half(pick, packed):
    packed = packed.astype(BF16)
    low = jnp.dot(pick[:, :HALF], packed, preferred_element_type=F32)
    high = jnp.dot(pick[:, HALF:], packed, preferred_element_type=F32)
    mixed = jnp.where(left_lanes(NB), low, high)
    return mixed + swap_lanes(mixed)


def half_adjoint_products(blocks_ref, h, picks, out_ref, add):
    row = lax.broadcasted_iota(jnp.int32, (GROUP, B), 0)
    side = jnp.where(left_lanes(GROUP), 0, 1)
    half = GROUP // 2
    rows = pl.ds(pl.multiple_of(h * (B // 2), B // 2), B // 2)
    for g in range(NB // GROUP):
        base = g * GROUP
        mine = picks[base : base + GROUP]
        lhs = jnp.concatenate(
            [jnp.where((row & (half - 1)) == q + side, mine, 0.0).astype(BF16) for q in range(0, half, 2)], axis=1
        )
        left = jnp.concatenate([blocks_ref[base + q, rows] for q in range(half)], axis=0)
        right = jnp.concatenate([blocks_ref[base + half + q, rows] for q in range(half)], axis=0)
        res = jnp.dot(lhs, jnp.concatenate([left, right], axis=1), preferred_element_type=F32)
        res = jnp.where(row < half, res[:, :B], res[:, B:])
        if add:
            res = res + out_ref[base : base + GROUP, :]
        out_ref[base : base + GROUP, :] = res


def half_forward_products(blk_t, h, picks, out_ref):
    wide = 2 * GROUP
    row = lax.broadcasted_iota(jnp.int32, (wide, B), 0)
    keep = ((lax.broadcasted_iota(jnp.int32, (GROUP, B), 0) < 8) & left_lanes(GROUP)) | (
        (lax.broadcasted_iota(jnp.int32, (GROUP, B), 0) >= 8) & ~left_lanes(GROUP)
    )
    for g in range(NB // wide):
        base = g * wide
        mine = picks[base : base + wide]
        lhs = jnp.concatenate([jnp.where((row & 7) == q, mine, 0.0).astype(BF16) for q in range(8)], axis=1)
        left = jnp.concatenate([blk_t[h, (g * 8 + q) * 2] for q in range(8)], axis=0)
        right = jnp.concatenate([blk_t[h, (g * 8 + q) * 2 + 1] for q in range(8)], axis=0)
        res = jnp.dot(lhs, jnp.concatenate([left, right], axis=1), preferred_element_type=F32)
        out_ref[base : base + GROUP, :] = jnp.where(keep, res[:GROUP, :B], 0.0)
        out_ref[base + GROUP : base + wide, :] = jnp.where(keep, res[GROUP:, B:], 0.0)


def pick_rows(pick, vector):
    return jnp.dot(pick, vector.astype(BF16), preferred_element_type=F32)


def scatter_rows(place, prod):
    high = prod.astype(BF16)
    low = (prod - high.astype(F32)).astype(BF16)
    return jnp.dot(place, high, preferred_element_type=F32) + jnp.dot(
        place, low, preferred_element_type=F32
    )


def lane_squares(vector):
    return jnp.sum(vector * vector, axis=0, keepdims=True)


def norm_of(parts):
    return jnp.sqrt(jnp.sum(parts, axis=(0, 1), keepdims=True) + EPS)


def kernel(
    blocks_hbm, rows_hbm, cols_hbm, counts_ref, data_hbm,
    out,
    blk, blk_t, rows_v, cols_v, pick_r, pick_c, place_r, place_c, prod,
    data, tb, wb, gsend, grecv, fsend, frecv, psend, precv, asend, arecv, bsend, brecv, scal,
    in_sem, blk_sem, g_ssem, g_rsem, w_ssem, w_rsem, f_ssem, f_rsem, p_ssem, p_rsem, t_ssem, t_rsem, a_ssem, a_rsem, b_ssem, b_rsem,
):
    r = lax.axis_index("row")
    c = lax.axis_index("col")
    x, z = r // NZ, r % NZ
    y, core = c // NC, c % NC
    row_peers = [((x + dx) % NX) * NZ + (z + dz) % NZ for dx, dz in ROW_STEPS]
    twin = y * NC + 1 - core
    y_peers = [((y + dy) % NY) * NC + core for dy in (2, 1, 3)]
    col_peers = [((y + dy) % NY) * NC + (core + dc) % NC for dy, dc in COL_STEPS]

    barrier = pltpu.get_barrier_semaphore()
    for p in row_peers:
        pl.semaphore_signal(barrier, inc=1, device_id=(p, c), device_id_type=MESH)
    for p in col_peers:
        pl.semaphore_signal(barrier, inc=1, device_id=(r, p), device_id_type=MESH)

    small = [
        pltpu.make_async_copy(rows_hbm, rows_v, in_sem.at[0]),
        pltpu.make_async_copy(cols_hbm, cols_v, in_sem.at[1]),
        pltpu.make_async_copy(data_hbm, data, in_sem.at[2]),
    ]
    for copy in small:
        copy.start()
    part = NB // LOADS
    loads = [
        pltpu.make_async_copy(
            blocks_hbm.at[0, 0, pl.ds(i * part, part)], blk.at[pl.ds(i * part, part)], blk_sem.at[i]
        )
        for i in range(LOADS)
    ]
    for copy in loads:
        copy.start()
    for copy in small:
        copy.wait()

    count = counts_ref[0, 0]
    sub = lax.broadcasted_iota(jnp.int32, (NB, NB), 0)
    lane = lax.broadcasted_iota(jnp.int32, (NB, NB), 1)
    live = lane < count

    def one_hot(index_ref):
        return (sub == index_ref[...]).astype(F32)

    hot_r = one_hot(rows_v)
    pick_r[...] = hot_r.T.astype(BF16)
    place_r[...] = jnp.where(live, hot_r, 0.0).astype(BF16)
    hot_c = one_hot(cols_v)
    pick_c[...] = hot_c.T.astype(BF16)
    place_c[...] = jnp.where(live, hot_c, 0.0).astype(BF16)

    def adjoint_place(squares):
        part = scatter_rows(place_c[...], prod[...])
        gsend[:, :RCH, :] = part.reshape(N_ROW, RCH, B)
        gsend[:, RCH:, :] = jnp.broadcast_to(squares.reshape(1, 1, B), (N_ROW, 1, B))

    def start_adjoint_send(it):
        for p in row_peers:
            pltpu.make_async_remote_copy(
                gsend.at[p], grecv.at[it, r], g_ssem, g_rsem.at[it], device_id=(p, c), device_id_type=MESH
            ).start()
        grecv[it, r] = gsend[r]

    def start_last_norm():
        asend[...] = lane_squares(wb[ITERS, r])
        for p in col_peers:
            pltpu.make_async_remote_copy(
                asend, arecv.at[c], a_ssem, a_rsem, device_id=(r, p), device_id_type=MESH
            ).start()
        arecv[c] = asend[...]
        others = arecv.at[pl.ds(0, N_COL - 1)]
        pltpu.make_async_copy(others, others, a_rsem).wait()
        bsend[...] = jnp.sum(arecv[...], axis=0)
        for p in row_peers:
            pltpu.make_async_remote_copy(
                bsend, brecv.at[r], b_ssem, b_rsem, device_id=(p, c), device_id_type=MESH
            ).start()
        brecv[r] = bsend[...]
        pltpu.make_async_copy(others, others, a_ssem).wait()

    def finish_adjoint(it, first):
        before = None if first else wb[it - 1, r] / scal[it - 1, 0:1, 0:1]
        got = grecv.at[it, pl.ds(0, N_ROW - 1)]
        pltpu.make_async_copy(got, got, g_rsem.at[it]).wait()
        total = jnp.sum(grecv[it], axis=0)
        beta = norm_of(total[RCH:])
        chunk = total[:RCH] / beta
        if not first:
            chunk = chunk - beta * before
        wb[it, r] = chunk
        scal[it, 1:2, :] = jnp.broadcast_to(beta, (1, B))
        for p in row_peers:
            pltpu.make_async_remote_copy(
                wb.at[it, r], wb.at[it, r], w_ssem, w_rsem.at[it], device_id=(p, c), device_id_type=MESH
            ).start()
        if not first:
            pl.when(it == ITERS)(start_last_norm)
        pltpu.make_async_copy(got, got, g_ssem).wait()
        landed = wb.at[it, pl.ds(0, N_ROW - 1)]
        pltpu.make_async_copy(landed, landed, w_rsem.at[it]).wait()
        pltpu.make_async_copy(landed, landed, w_ssem).wait()

    def forward_half(h, picks):
        half_forward_products(blk_t, h, picks, prod)
        both = scatter_rows(place_r[...], prod[...])
        both = both + swap_lanes(both)
        return jnp.where(left_lanes(HALF), both[:HALF], both[HALF:])

    def forward_and_adjoint(it):
        vec = wb[it].reshape(NB, B)
        picks = pick_rows(pick_c[...], vec)
        squares = lane_squares(vec)
        fsend[:HALF, :] = forward_half(1 - core, picks)
        fsend[HALF:, :] = squares
        pair = pltpu.make_async_remote_copy(
            fsend, frecv.at[it], f_ssem, f_rsem.at[it], device_id=(r, twin), device_id_type=MESH
        )
        pair.start()
        psend[:HALF, :] = forward_half(core, picks)
        psend[HALF:, :] = squares
        pair.wait()
        psend[...] = psend[...] + frecv[it]
        for p in y_peers:
            pltpu.make_async_remote_copy(
                psend, precv.at[it, y], p_ssem, p_rsem.at[it], device_id=(r, p), device_id_type=MESH
            ).start()
        precv[it, y] = psend[...]
        unit = tb[it, core] / scal[it, 1:2, 0:1]
        got = precv.at[it, pl.ds(0, NY - 1)]
        pltpu.make_async_copy(got, got, p_rsem.at[it]).wait()
        total = jnp.sum(precv[it], axis=0)
        alpha = norm_of(total[HALF:])
        tb[it + 1, core] = total[:HALF] / alpha - alpha * unit
        done = pltpu.make_async_remote_copy(
            tb.at[it + 1, core], tb.at[it + 1, core], t_ssem, t_rsem.at[it],
            device_id=(r, twin), device_id_type=MESH,
        )
        done.start()
        scal[it, 0:1, :] = jnp.broadcast_to(alpha, (1, B))
        half_adjoint_products(blk, core, pick_half(pick_r[...], tb[it + 1, core]), prod, False)
        pltpu.make_async_copy(got, got, p_ssem).wait()
        done.wait()
        half_adjoint_products(blk, 1 - core, pick_half(pick_r[...], tb[it + 1, 1 - core]), prod, True)
        adjoint_place(lane_squares(tb[it + 1, 0]) + lane_squares(tb[it + 1, 1]))

    block_products(blk, pick_rows(pick_r[...], data[...]), prod, loads)
    adjoint_place(lane_squares(data[...]))
    pl.semaphore_wait(barrier, N_ROW + N_COL - 2)
    start_adjoint_send(0)
    tb[0, 0], tb[0, 1] = halves(data[...])

    def transpose_pair(n, carry):
        first = (n // 16) * 32 + (n % 2) * 16 + (n // 2) % 8
        for h in range(2):
            rows = slice(h * (B // 2), (h + 1) * (B // 2))
            blk_t[h, n] = jnp.concatenate([blk[first, rows], blk[first + 8, rows]], axis=0).T
        return carry

    lax.fori_loop(0, NB // 2, transpose_pair, 0, unroll=8)
    finish_adjoint(0, True)

    def step(it, carry):
        forward_and_adjoint(it)
        start_adjoint_send(it + 1)
        finish_adjoint(it + 1, False)
        return carry

    lax.fori_loop(0, ITERS, step, 0)

    alphas = [scal[i, 0:1, 0:1] for i in range(ITERS)]
    betas = [scal[i, 1:2, 0:1] for i in range(ITERS + 1)]
    top, bottom = whole(tb[ITERS, 0] / betas[ITERS], tb[ITERS, 1] / betas[ITERS])
    out[2, :HALF] = top
    out[2, HALF:] = bottom
    search = wb[0].reshape(NB, B) / alphas[0]
    answer = jnp.zeros((NB, B), F32)
    phibar, rhobar = betas[0], alphas[0]
    for i in range(ITERS):
        beta = betas[i + 1]
        rho = jnp.sqrt(rhobar * rhobar + beta * beta)
        cosine, sine = rhobar / rho, beta / rho
        phi = cosine * phibar
        phibar = sine * phibar
        answer = answer + (phi / rho) * search
        if i + 1 < ITERS:
            theta = sine * alphas[i + 1]
            rhobar = -cosine * alphas[i + 1]
            search = wb[i + 1].reshape(NB, B) / alphas[i + 1] - (theta / rho) * search
    out[0] = answer
    others = brecv.at[pl.ds(0, N_ROW - 1)]
    pltpu.make_async_copy(others, others, b_rsem).wait()
    alpha = norm_of(jnp.sum(brecv[...], axis=0))
    out[1] = wb[ITERS].reshape(NB, B) / alpha - (sine * alpha / rho) * search
    pltpu.make_async_copy(others, others, b_ssem).wait()


def per_device(blocks, block_rows, block_cols, counts, data):
    vec = jax.ShapeDtypeStruct((NB, B), F32)
    hbm = pl.BlockSpec(memory_space=pl.ANY)

    def in_hbm(a):
        return pltpu.with_memory_space_constraint(a, pltpu.HBM)

    out = pl.pallas_call(
        kernel,
        out_shape=jax.ShapeDtypeStruct((3, NB, B), F32),
        in_specs=[hbm, hbm, hbm, pl.BlockSpec(memory_space=pltpu.SMEM), hbm],
        out_specs=pl.BlockSpec(memory_space=pltpu.VMEM),
        scratch_shapes=[
            pltpu.VMEM((NB, B, B), BF16),
            pltpu.VMEM((2, NB // 2, B, B), BF16),
            pltpu.VMEM((1, NB), jnp.int32),
            pltpu.VMEM((1, NB), jnp.int32),
            pltpu.VMEM((NB, NB), BF16),
            pltpu.VMEM((NB, NB), BF16),
            pltpu.VMEM((NB, NB), BF16),
            pltpu.VMEM((NB, NB), BF16),
            pltpu.VMEM((NB, B), F32),
            pltpu.VMEM((NB, B), F32),
            pltpu.VMEM((ITERS + 1, 2, HALF, B), F32),
            pltpu.VMEM((ITERS + 1, N_ROW, RCH, B), F32),
            pltpu.VMEM((N_ROW, RCH + 1, B), F32),
            pltpu.VMEM((ITERS + 1, N_ROW, RCH + 1, B), F32),
            pltpu.VMEM((HALF + 1, B), F32),
            pltpu.VMEM((ITERS, HALF + 1, B), F32),
            pltpu.VMEM((HALF + 1, B), F32),
            pltpu.VMEM((ITERS, NY, HALF + 1, B), F32),
            pltpu.VMEM((1, B), F32),
            pltpu.VMEM((N_COL, 1, B), F32),
            pltpu.VMEM((1, B), F32),
            pltpu.VMEM((N_ROW, 1, B), F32),
            pltpu.VMEM((ITERS + 1, 8, B), F32),
            pltpu.SemaphoreType.DMA((3,)),
            pltpu.SemaphoreType.DMA((LOADS,)),
            pltpu.SemaphoreType.DMA,
            pltpu.SemaphoreType.DMA((ITERS + 1,)),
            pltpu.SemaphoreType.DMA,
            pltpu.SemaphoreType.DMA((ITERS + 1,)),
            pltpu.SemaphoreType.DMA,
            pltpu.SemaphoreType.DMA((ITERS,)),
            pltpu.SemaphoreType.DMA,
            pltpu.SemaphoreType.DMA((ITERS,)),
            pltpu.SemaphoreType.DMA,
            pltpu.SemaphoreType.DMA((ITERS,)),
            pltpu.SemaphoreType.DMA,
            pltpu.SemaphoreType.DMA,
            pltpu.SemaphoreType.DMA,
            pltpu.SemaphoreType.DMA,
        ],
        compiler_params=pltpu.CompilerParams(
            collective_id=0, has_side_effects=True, vmem_limit_bytes=53000 * 1024
        ),
        name="lsqr",
    )(blocks, in_hbm(block_rows[0]), in_hbm(block_cols[0]), counts, in_hbm(data.reshape(NB, B)))
    return out[0].reshape(-1), out[1].reshape(-1), out[2].reshape(-1)


def solution(mesh):
    return jax.shard_map(
        per_device,
        mesh=mesh,
        in_specs=(
            P("row", "col", None, None, None),
            P("row", "col", None),
            P("row", "col", None),
            P("row", "col"),
            P("row"),
        ),
        out_specs=(P("col"), P("col"), P("row")),
        check_vma=False,
    )
```

```python
import jax
import jax.numpy as jnp
from jax import lax
from jax.experimental import pallas as pl
from jax.experimental.pallas import tpu as pltpu
from jax.sharding import PartitionSpec as P

MESH = pl.DeviceIdType.MESH
F32 = jnp.float32
BF16 = jnp.bfloat16
EPS = 1e-06
ITERS = 3
B = 128
NB = 256
NX, NZ, NY, NC = 4, 8, 4, 2
N_ROW = NX * NZ
N_COL = NY * NC
RCH = NB // N_ROW
LOADS = 8
HALF = NB // NC
GROUP = 16


def ring(step, size):
    return min(step, size - step)


ROW_STEPS = sorted(
    ((dx, dz) for dx in range(NX) for dz in range(NZ) if dx or dz),
    key=lambda s: -(ring(s[0], NX) + ring(s[1], NZ)),
)

COL_STEPS = sorted(
    ((dy, dc) for dy in range(NY) for dc in range(NC) if dy or dc),
    key=lambda s: -(2 * ring(s[0], NY) + s[1]),
)


def block_products(blocks_ref, picks, out_ref, loads=()):
    row = lax.broadcasted_iota(jnp.int32, (GROUP, B), 0)
    half = GROUP // 2
    for g in range(NB // GROUP):
        base = g * GROUP
        if loads and base % (NB // LOADS) == 0:
            loads[base * LOADS // NB].wait()
        mine = picks[base : base + GROUP]
        lhs = jnp.concatenate(
            [jnp.where((row & (half - 1)) == q, mine, 0.0).astype(BF16) for q in range(half)], axis=1
        )
        left = jnp.concatenate([blocks_ref[base + q] for q in range(half)], axis=0)
        right = jnp.concatenate([blocks_ref[base + half + q] for q in range(half)], axis=0)
        rhs = jnp.concatenate([left, right], axis=1)
        res = jnp.dot(lhs, rhs, preferred_element_type=F32)
        out_ref[base : base + GROUP, :] = jnp.where(row < half, res[:, :B], res[:, B:])


def swap_lanes(a):
    return jnp.concatenate([a[:, B // 2 :], a[:, : B // 2]], axis=1)


def left_lanes(rows):
    return lax.broadcasted_iota(jnp.int32, (rows, B), 1) < B // 2


def halves(vector):
    low, high = vector[:HALF], vector[HALF:]
    left = left_lanes(HALF)
    return jnp.where(left, low, swap_lanes(high)), jnp.where(left, swap_lanes(low), high)


def whole(first, second):
    left = left_lanes(HALF)
    return jnp.where(left, first, swap_lanes(second)), jnp.where(left, swap_lanes(first), second)


def pick_half(pick, packed):
    packed = packed.astype(BF16)
    low = jnp.dot(pick[:, :HALF], packed, preferred_element_type=F32)
    high = jnp.dot(pick[:, HALF:], packed, preferred_element_type=F32)
    mixed = jnp.where(left_lanes(NB), low, high)
    return mixed + swap_lanes(mixed)


def half_adjoint_products(blocks_ref, h, picks, out_ref, add):
    row = lax.broadcasted_iota(jnp.int32, (GROUP, B), 0)
    side = jnp.where(left_lanes(GROUP), 0, 1)
    half = GROUP // 2
    rows = pl.ds(pl.multiple_of(h * (B // 2), B // 2), B // 2)
    for g in range(NB // GROUP):
        base = g * GROUP
        mine = picks[base : base + GROUP]
        lhs = jnp.concatenate(
            [jnp.where((row & (half - 1)) == q + side, mine, 0.0).astype(BF16) for q in range(0, half, 2)], axis=1
        )
        left = jnp.concatenate([blocks_ref[base + q, rows] for q in range(half)], axis=0)
        right = jnp.concatenate([blocks_ref[base + half + q, rows] for q in range(half)], axis=0)
        res = jnp.dot(lhs, jnp.concatenate([left, right], axis=1), preferred_element_type=F32)
        res = jnp.where(row < half, res[:, :B], res[:, B:])
        if add:
            res = res + out_ref[base : base + GROUP, :]
        out_ref[base : base + GROUP, :] = res


def half_forward_products(blk_t, h, picks, out_ref):
    wide = 2 * GROUP
    row = lax.broadcasted_iota(jnp.int32, (wide, B), 0)
    keep = ((lax.broadcasted_iota(jnp.int32, (GROUP, B), 0) < 8) & left_lanes(GROUP)) | (
        (lax.broadcasted_iota(jnp.int32, (GROUP, B), 0) >= 8) & ~left_lanes(GROUP)
    )
    for g in range(NB // wide):
        base = g * wide
        mine = picks[base : base + wide]
        lhs = jnp.concatenate([jnp.where((row & 7) == q, mine, 0.0).astype(BF16) for q in range(8)], axis=1)
        left = jnp.concatenate([blk_t[h, (g * 8 + q) * 2] for q in range(8)], axis=0)
        right = jnp.concatenate([blk_t[h, (g * 8 + q) * 2 + 1] for q in range(8)], axis=0)
        res = jnp.dot(lhs, jnp.concatenate([left, right], axis=1), preferred_element_type=F32)
        out_ref[base : base + GROUP, :] = jnp.where(keep, res[:GROUP, :B], 0.0)
        out_ref[base + GROUP : base + wide, :] = jnp.where(keep, res[GROUP:, B:], 0.0)


def pick_rows(pick, vector):
    return jnp.dot(pick, vector.astype(BF16), preferred_element_type=F32)


def scatter_rows(place, prod):
    high = prod.astype(BF16)
    low = (prod - high.astype(F32)).astype(BF16)
    return jnp.dot(place, high, preferred_element_type=F32) + jnp.dot(
        place, low, preferred_element_type=F32
    )


def lane_squares(vector):
    return jnp.sum(vector * vector, axis=0, keepdims=True)


def norm_of(parts):
    return jnp.sqrt(jnp.sum(parts, axis=(0, 1), keepdims=True) + EPS)


def kernel(
    blocks_hbm, rows_hbm, cols_hbm, counts_ref, data_hbm,
    out,
    blk, blk_t, rows_v, cols_v, pick_r, pick_c, place_r, place_c, prod,
    data, tb, wb, gsend, grecv, fsend, frecv, psend, precv, asend, arecv, bsend, brecv, scal,
    in_sem, blk_sem, g_ssem, g_rsem, w_ssem, w_rsem, f_ssem, f_rsem, p_ssem, p_rsem, t_ssem, t_rsem, a_ssem, a_rsem, b_ssem, b_rsem,
):
    r = lax.axis_index("row")
    c = lax.axis_index("col")
    x, z = r // NZ, r % NZ
    y, core = c // NC, c % NC
    row_peers = [((x + dx) % NX) * NZ + (z + dz) % NZ for dx, dz in ROW_STEPS]
    twin = y * NC + 1 - core
    y_peers = [((y + dy) % NY) * NC + core for dy in (2, 1, 3)]
    col_peers = [((y + dy) % NY) * NC + (core + dc) % NC for dy, dc in COL_STEPS]

    barrier = pltpu.get_barrier_semaphore()
    for p in row_peers:
        pl.semaphore_signal(barrier, inc=1, device_id=(p, c), device_id_type=MESH)
    for p in col_peers:
        pl.semaphore_signal(barrier, inc=1, device_id=(r, p), device_id_type=MESH)

    small = [
        pltpu.make_async_copy(rows_hbm, rows_v, in_sem.at[0]),
        pltpu.make_async_copy(cols_hbm, cols_v, in_sem.at[1]),
        pltpu.make_async_copy(data_hbm, data, in_sem.at[2]),
    ]
    for copy in small:
        copy.start()
    part = NB // LOADS
    loads = [
        pltpu.make_async_copy(
            blocks_hbm.at[0, 0, pl.ds(i * part, part)], blk.at[pl.ds(i * part, part)], blk_sem.at[i]
        )
        for i in range(LOADS)
    ]
    for copy in loads:
        copy.start()
    for copy in small:
        copy.wait()

    count = counts_ref[0, 0]
    sub = lax.broadcasted_iota(jnp.int32, (NB, NB), 0)
    lane = lax.broadcasted_iota(jnp.int32, (NB, NB), 1)
    live = lane < count

    def one_hot(index_ref):
        return (sub == index_ref[...]).astype(F32)

    pick_r[...] = one_hot(rows_v).T.astype(BF16)
    place_c[...] = jnp.where(live, one_hot(cols_v), 0.0).astype(BF16)

    def adjoint_place(squares):
        part = scatter_rows(place_c[...], prod[...])
        gsend[:, :RCH, :] = part.reshape(N_ROW, RCH, B)
        gsend[:, RCH:, :] = jnp.broadcast_to(squares.reshape(1, 1, B), (N_ROW, 1, B))

    def start_adjoint_send(it):
        for p in row_peers:
            pltpu.make_async_remote_copy(
                gsend.at[p], grecv.at[it, r], g_ssem, g_rsem.at[it], device_id=(p, c), device_id_type=MESH
            ).start()
        grecv[it, r] = gsend[r]

    def start_last_norm():
        asend[...] = lane_squares(wb[ITERS, r])
        for p in col_peers:
            pltpu.make_async_remote_copy(
                asend, arecv.at[c], a_ssem, a_rsem, device_id=(r, p), device_id_type=MESH
            ).start()
        arecv[c] = asend[...]
        others = arecv.at[pl.ds(0, N_COL - 1)]
        pltpu.make_async_copy(others, others, a_rsem).wait()
        bsend[...] = jnp.sum(arecv[...], axis=0)
        for p in row_peers:
            pltpu.make_async_remote_copy(
                bsend, brecv.at[r], b_ssem, b_rsem, device_id=(p, c), device_id_type=MESH
            ).start()
        brecv[r] = bsend[...]
        pltpu.make_async_copy(others, others, a_ssem).wait()

    def finish_adjoint(it, first):
        before = None if first else wb[it - 1, r] / scal[it - 1, 0:1, 0:1]
        got = grecv.at[it, pl.ds(0, N_ROW - 1)]
        pltpu.make_async_copy(got, got, g_rsem.at[it]).wait()
        total = jnp.sum(grecv[it], axis=0)
        beta = norm_of(total[RCH:])
        chunk = total[:RCH] / beta
        if not first:
            chunk = chunk - beta * before
        wb[it, r] = chunk
        scal[it, 1:2, :] = jnp.broadcast_to(beta, (1, B))
        for p in row_peers:
            pltpu.make_async_remote_copy(
                wb.at[it, r], wb.at[it, r], w_ssem, w_rsem.at[it], device_id=(p, c), device_id_type=MESH
            ).start()
        if not first:
            pl.when(it == ITERS)(start_last_norm)
        pltpu.make_async_copy(got, got, g_ssem).wait()
        landed = wb.at[it, pl.ds(0, N_ROW - 1)]
        pltpu.make_async_copy(landed, landed, w_rsem.at[it]).wait()
        pltpu.make_async_copy(landed, landed, w_ssem).wait()

    def forward_half(h, picks):
        half_forward_products(blk_t, h, picks, prod)
        both = scatter_rows(place_r[...], prod[...])
        both = both + swap_lanes(both)
        return jnp.where(left_lanes(HALF), both[:HALF], both[HALF:])

    def forward_and_adjoint(it):
        vec = wb[it].reshape(NB, B)
        picks = pick_rows(pick_c[...], vec)
        squares = lane_squares(vec)
        fsend[:HALF, :] = forward_half(1 - core, picks)
        fsend[HALF:, :] = squares
        pair = pltpu.make_async_remote_copy(
            fsend, frecv.at[it], f_ssem, f_rsem.at[it], device_id=(r, twin), device_id_type=MESH
        )
        pair.start()
        psend[:HALF, :] = forward_half(core, picks)
        psend[HALF:, :] = squares
        pair.wait()
        psend[...] = psend[...] + frecv[it]
        for p in y_peers:
            pltpu.make_async_remote_copy(
                psend, precv.at[it, y], p_ssem, p_rsem.at[it], device_id=(r, p), device_id_type=MESH
            ).start()
        precv[it, y] = psend[...]
        unit = tb[it, core] / scal[it, 1:2, 0:1]
        got = precv.at[it, pl.ds(0, NY - 1)]
        pltpu.make_async_copy(got, got, p_rsem.at[it]).wait()
        total = jnp.sum(precv[it], axis=0)
        alpha = norm_of(total[HALF:])
        tb[it + 1, core] = total[:HALF] / alpha - alpha * unit
        done = pltpu.make_async_remote_copy(
            tb.at[it + 1, core], tb.at[it + 1, core], t_ssem, t_rsem.at[it],
            device_id=(r, twin), device_id_type=MESH,
        )
        done.start()
        scal[it, 0:1, :] = jnp.broadcast_to(alpha, (1, B))
        half_adjoint_products(blk, core, pick_half(pick_r[...], tb[it + 1, core]), prod, False)
        pltpu.make_async_copy(got, got, p_ssem).wait()
        done.wait()
        half_adjoint_products(blk, 1 - core, pick_half(pick_r[...], tb[it + 1, 1 - core]), prod, True)
        adjoint_place(lane_squares(tb[it + 1, 0]) + lane_squares(tb[it + 1, 1]))

    block_products(blk, pick_rows(pick_r[...], data[...]), prod, loads)
    adjoint_place(lane_squares(data[...]))
    pl.semaphore_wait(barrier, N_ROW + N_COL - 2)
    start_adjoint_send(0)
    tb[0, 0], tb[0, 1] = halves(data[...])

    def transpose_pair(n, carry):
        first = (n // 16) * 32 + (n % 2) * 16 + (n // 2) % 8
        for h in range(2):
            rows = slice(h * (B // 2), (h + 1) * (B // 2))
            blk_t[h, n] = jnp.concatenate([blk[first, rows], blk[first + 8, rows]], axis=0).T
        return carry

    pick_c[...] = one_hot(cols_v).T.astype(BF16)
    place_r[...] = jnp.where(live, one_hot(rows_v), 0.0).astype(BF16)
    lax.fori_loop(0, NB // 2, transpose_pair, 0, unroll=8)
    finish_adjoint(0, True)

    def step(it, carry):
        forward_and_adjoint(it)
        start_adjoint_send(it + 1)
        finish_adjoint(it + 1, False)
        return carry

    lax.fori_loop(0, ITERS, step, 0)

    alphas = [scal[i, 0:1, 0:1] for i in range(ITERS)]
    betas = [scal[i, 1:2, 0:1] for i in range(ITERS + 1)]
    top, bottom = whole(tb[ITERS, 0] / betas[ITERS], tb[ITERS, 1] / betas[ITERS])
    out[2, :HALF] = top
    out[2, HALF:] = bottom
    search = wb[0].reshape(NB, B) / alphas[0]
    answer = jnp.zeros((NB, B), F32)
    phibar, rhobar = betas[0], alphas[0]
    for i in range(ITERS):
        beta = betas[i + 1]
        rho = jnp.sqrt(rhobar * rhobar + beta * beta)
        cosine, sine = rhobar / rho, beta / rho
        phi = cosine * phibar
        phibar = sine * phibar
        answer = answer + (phi / rho) * search
        if i + 1 < ITERS:
            theta = sine * alphas[i + 1]
            rhobar = -cosine * alphas[i + 1]
            search = wb[i + 1].reshape(NB, B) / alphas[i + 1] - (theta / rho) * search
    out[0] = answer
    others = brecv.at[pl.ds(0, N_ROW - 1)]
    pltpu.make_async_copy(others, others, b_rsem).wait()
    alpha = norm_of(jnp.sum(brecv[...], axis=0))
    out[1] = wb[ITERS].reshape(NB, B) / alpha - (sine * alpha / rho) * search
    pltpu.make_async_copy(others, others, b_ssem).wait()


def per_device(blocks, block_rows, block_cols, counts, data):
    vec = jax.ShapeDtypeStruct((NB, B), F32)
    hbm = pl.BlockSpec(memory_space=pl.ANY)

    def in_hbm(a):
        return pltpu.with_memory_space_constraint(a, pltpu.HBM)

    out = pl.pallas_call(
        kernel,
        out_shape=jax.ShapeDtypeStruct((3, NB, B), F32),
        in_specs=[hbm, hbm, hbm, pl.BlockSpec(memory_space=pltpu.SMEM), hbm],
        out_specs=pl.BlockSpec(memory_space=pltpu.VMEM),
        scratch_shapes=[
            pltpu.VMEM((NB, B, B), BF16),
            pltpu.VMEM((2, NB // 2, B, B), BF16),
            pltpu.VMEM((1, NB), jnp.int32),
            pltpu.VMEM((1, NB), jnp.int32),
            pltpu.VMEM((NB, NB), BF16),
            pltpu.VMEM((NB, NB), BF16),
            pltpu.VMEM((NB, NB), BF16),
            pltpu.VMEM((NB, NB), BF16),
            pltpu.VMEM((NB, B), F32),
            pltpu.VMEM((NB, B), F32),
            pltpu.VMEM((ITERS + 1, 2, HALF, B), F32),
            pltpu.VMEM((ITERS + 1, N_ROW, RCH, B), F32),
            pltpu.VMEM((N_ROW, RCH + 1, B), F32),
            pltpu.VMEM((ITERS + 1, N_ROW, RCH + 1, B), F32),
            pltpu.VMEM((HALF + 1, B), F32),
            pltpu.VMEM((ITERS, HALF + 1, B), F32),
            pltpu.VMEM((HALF + 1, B), F32),
            pltpu.VMEM((ITERS, NY, HALF + 1, B), F32),
            pltpu.VMEM((1, B), F32),
            pltpu.VMEM((N_COL, 1, B), F32),
            pltpu.VMEM((1, B), F32),
            pltpu.VMEM((N_ROW, 1, B), F32),
            pltpu.VMEM((ITERS + 1, 8, B), F32),
            pltpu.SemaphoreType.DMA((3,)),
            pltpu.SemaphoreType.DMA((LOADS,)),
            pltpu.SemaphoreType.DMA,
            pltpu.SemaphoreType.DMA((ITERS + 1,)),
            pltpu.SemaphoreType.DMA,
            pltpu.SemaphoreType.DMA((ITERS + 1,)),
            pltpu.SemaphoreType.DMA,
            pltpu.SemaphoreType.DMA((ITERS,)),
            pltpu.SemaphoreType.DMA,
            pltpu.SemaphoreType.DMA((ITERS,)),
            pltpu.SemaphoreType.DMA,
            pltpu.SemaphoreType.DMA((ITERS,)),
            pltpu.SemaphoreType.DMA,
            pltpu.SemaphoreType.DMA,
            pltpu.SemaphoreType.DMA,
            pltpu.SemaphoreType.DMA,
        ],
        compiler_params=pltpu.CompilerParams(
            collective_id=0, has_side_effects=True, vmem_limit_bytes=53000 * 1024
        ),
        name="lsqr",
    )(blocks, in_hbm(block_rows[0]), in_hbm(block_cols[0]), counts, in_hbm(data.reshape(NB, B)))
    return out[0].reshape(-1), out[1].reshape(-1), out[2].reshape(-1)


def solution(mesh):
    return jax.shard_map(
        per_device,
        mesh=mesh,
        in_specs=(
            P("row", "col", None, None, None),
            P("row", "col", None),
            P("row", "col", None),
            P("row", "col"),
            P("row"),
        ),
        out_specs=(P("col"), P("col"), P("row")),
        check_vma=False,
    )
```
